32 devices in a mesh: dp: 8 (over z, x), tensor: 4 (over y, core).
Axes of the slice: x: 2, y: 2, z: 4, core: 2. Of those that a mesh axis runs over, the one named last changes fastest.
Arguments:
- tokens: bfloat16 [16384, 1024], P('dp'), may hold values from -6 to 6
- cotangent: bfloat16 [16384, 1024], P(('dp', 'tensor')), may hold values from -6 to 6
- norm1_gain: float32 [1024], replicated, may hold values from 0.5 to 1.5
- norm2_gain: float32 [1024], replicated, may hold values from 0.5 to 1.5
- query_weight: bfloat16 [1024, 1024], P('dp', 'tensor'), may hold values from -0.1875 to 0.1875
- key_weight: bfloat16 [1024, 1024], P('dp', 'tensor'), may hold values from -0.1875 to 0.1875
- value_weight: bfloat16 [1024, 2048], P('dp', 'tensor'), may hold values from -0.1875 to 0.1875
- outgate_weight: bfloat16 [1024, 2048], P('dp', 'tensor'), may hold values from -0.1875 to 0.1875
- alpha_weight: bfloat16 [1024, 8], P('dp', 'tensor'), may hold values from -0.1875 to 0.1875
- beta_weight: bfloat16 [1024, 8], P('dp', 'tensor'), may hold values from -0.1875 to 0.1875
- conv_query: float32 [4, 1024], P(None, 'tensor'), may hold values from -3 to 3
- conv_key: float32 [4, 1024], P(None, 'tensor'), may hold values from -3 to 3
- conv_value: float32 [4, 2048], P(None, 'tensor'), may hold values from -3 to 3
- decay_log: float32 [8], P('tensor'), may hold values from 0 to 2.77
- decay_bias: float32 [8], P('tensor'), may hold values from -4.6 to -2.3
- onorm_gain: float32 [256], replicated, may hold values from 0.5 to 1.5
- output_weight: bfloat16 [2048, 1024], P('tensor', 'dp'), may hold values from -0.25 to 0.25
- gate_weight: bfloat16 [1024, 2816], P('dp', 'tensor'), may hold values from -0.1875 to 0.1875
- up_weight: bfloat16 [1024, 2816], P('dp', 'tensor'), may hold values from -0.1875 to 0.1875
- down_weight: bfloat16 [2816, 1024], P('tensor', 'dp'), may hold values from -0.109375 to 0.109375
Outputs:
- block_output: bfloat16 [16384, 1024], P(('dp', 'tensor'))
- tokens_grad: float32 [16384, 1024], P(('dp', 'tensor'))
- norm1_gain_grad: float32 [1024], P('tensor')
- norm2_gain_grad: float32 [1024], P('tensor')
- query_weight_grad: float32 [1024, 1024], P('dp', 'tensor')
- key_weight_grad: float32 [1024, 1024], P('dp', 'tensor')
- value_weight_grad: float32 [1024, 2048], P('dp', 'tensor')
- outgate_weight_grad: float32 [1024, 2048], P('dp', 'tensor')
- alpha_weight_grad: float32 [1024, 8], P('dp', 'tensor')
- beta_weight_grad: float32 [1024, 8], P('dp', 'tensor')
- conv_query_grad: float32 [4, 1024], P(None, 'tensor')
- conv_key_grad: float32 [4, 1024], P(None, 'tensor')
- conv_value_grad: float32 [4, 2048], P(None, 'tensor')
- decay_log_grad: float32 [8], P('tensor')
- decay_bias_grad: float32 [8], P('tensor')
- onorm_gain_grad: float32 [256], P('tensor')
- output_weight_grad: float32 [2048, 1024], P('tensor', 'dp')
- gate_weight_grad: float32 [1024, 2816], P('dp', 'tensor')
- up_weight_grad: float32 [1024, 2816], P('dp', 'tensor')
- down_weight_grad: float32 [2816, 1024], P('tensor', 'dp')
The draws below stay inside these ranges and needn't reach their ends.
All inputs are finite; a program needn't handle non-finite values.
Results may differ from the reference program's by a relative error of at most 0.012.
Values may be sent and summed in bfloat16 or wider, within the bound.
No kernel may reach another device: no remote copies, remote signals or barrier semaphores. Data moves between devices by JAX's collectives and lax.ppermute only.
A program may use at most 384 MiB of HBM per device.

```python
import math
import jax
import jax.numpy as jnp
from jax import lax

D = 1024
HEADS = 8
DK = 128
DV = 256
FF = 2816
KERNEL = 4
STRETCH = 64
SEQ = 2048
TOKENS = 16384


def level_of(own_key, extent, split, least, high):
    def one(position, shards_of):
        heights = jax.random.uniform(jax.random.fold_in(jax.random.fold_in(own_key, 6), position), (shards_of,), jnp.float32, least / len(split), high / len(split))
        return jnp.repeat(jnp.exp(heights), extent[position] // shards_of).reshape((-1,) + (1,) * (len(extent) - position - 1))

    level = one(*split[0])
    for cut in split[1:]:
        level = level * one(*cut)
    return level


def scatter_about(rng, extent, width, bound, pieces=(), kind=jnp.bfloat16):
    values = jax.random.normal(rng, extent, jnp.float32) * width
    if len(pieces) > 0:
        values = level_of(rng, extent, pieces, -0.22, 0.18) * values
    return jnp.clip(values, min=-bound, max=bound).astype(kind)


def setup_inputs(seed: int = 0) -> dict:
    key_list = jax.random.split(jax.random.key(seed), 21)
    tokens = scatter_about(key_list[0], (TOKENS, D), 1.0, 6.0, ((0, 8),))
    cotangent = scatter_about(key_list[1], (TOKENS, D), 1.0, 6.0, ((0, 32),))
    norm1_gain = jnp.clip(1.0 + 0.1 * jax.random.normal(key_list[2], (D,), jnp.float32), 0.5, 1.5)
    norm2_gain = jnp.clip(1.0 + 0.1 * jax.random.normal(key_list[3], (D,), jnp.float32), 0.5, 1.5)
    query_weight = scatter_about(key_list[4], (D, HEADS * DK), D ** -0.5, 0.1875, ((0, 8), (1, 4)))
    key_weight = scatter_about(key_list[5], (D, HEADS * DK), D ** -0.5, 0.1875, ((0, 8), (1, 4)))
    value_weight = scatter_about(key_list[6], (D, HEADS * DV), D ** -0.5, 0.1875, ((0, 8), (1, 4)))
    outgate_weight = scatter_about(key_list[7], (D, HEADS * DV), D ** -0.5, 0.1875, ((0, 8), (1, 4)))
    alpha_weight = scatter_about(key_list[8], (D, HEADS), D ** -0.5, 0.1875, ((0, 8), (1, 4)))
    beta_weight = scatter_about(key_list[9], (D, HEADS), D ** -0.5, 0.1875, ((0, 8), (1, 4)))
    conv_query = scatter_about(key_list[10], (KERNEL, HEADS * DK), KERNEL ** -0.5, 3.0, ((1, 4),), jnp.float32)
    conv_key = scatter_about(key_list[11], (KERNEL, HEADS * DK), KERNEL ** -0.5, 3.0, ((1, 4),), jnp.float32)
    conv_value = scatter_about(key_list[12], (KERNEL, HEADS * DV), KERNEL ** -0.5, 3.0, ((1, 4),), jnp.float32)
    decay_log = jnp.clip(2.77 * jax.random.uniform(key_list[13], (HEADS,), jnp.float32) ** level_of(key_list[13], (HEADS,), ((0, 4),), -0.2, 0.2), 0.0, 2.77)
    decay_bias = jnp.clip(-4.6 + 2.3 * jax.random.uniform(key_list[14], (HEADS,), jnp.float32) ** level_of(key_list[14], (HEADS,), ((0, 4),), -0.2, 0.2), -4.6, -2.3)
    onorm_gain = jnp.clip(1.0 + 0.1 * jax.random.normal(key_list[15], (DV,), jnp.float32), 0.5, 1.5)
    output_weight = scatter_about(key_list[16], (HEADS * DV, D), (HEADS * DV // 4) ** -0.5, 0.25, ((0, 4), (1, 8)))
    gate_weight = scatter_about(key_list[17], (D, FF), D ** -0.5, 0.1875, ((0, 8), (1, 4)))
    up_weight = scatter_about(key_list[18], (D, FF), D ** -0.5, 0.1875, ((0, 8), (1, 4)))
    down_weight = scatter_about(key_list[19], (FF, D), FF ** -0.5, 0.109375, ((0, 4), (1, 8)))
    return {"tokens": tokens, "cotangent": cotangent, "norm1_gain": norm1_gain, "norm2_gain": norm2_gain, "query_weight": query_weight, "key_weight": key_weight, "value_weight": value_weight, "outgate_weight": outgate_weight, "alpha_weight": alpha_weight, "beta_weight": beta_weight, "conv_query": conv_query, "conv_key": conv_key, "conv_value": conv_value, "decay_log": decay_log, "decay_bias": decay_bias, "onorm_gain": onorm_gain, "output_weight": output_weight, "gate_weight": gate_weight, "up_weight": up_weight, "down_weight": down_weight}


HIGH = lax.Precision.HIGHEST
EPS_NORM = 1e-05

@jax.custom_vjp
def low(v):
    return lax.optimization_barrier(v.astype(jnp.bfloat16)).astype(jnp.float32)

@jax.custom_vjp
def low_back(v):
    return v

def low_keep(v):
    return (low(v), None)

def low_pass(kept, grad):
    return (grad,)

def back_keep(v):
    return (v, None)

def back_low(kept, grad):
    return (low(grad),)
low.defvjp(low_keep, low_pass)
low_back.defvjp(back_keep, back_low)

def matmul_high(left_side, right_side):
    return jnp.einsum('...ij,...jk->...ik', left_side, right_side, precision=HIGH)

def norm_one(inputs, gain):
    return inputs * lax.rsqrt(lax.optimization_barrier(jnp.mean(inputs * inputs, axis=-1, keepdims=True)) + EPS_NORM) * gain

def unit_rows(inputs):
    return inputs * lax.rsqrt(lax.optimization_barrier(jnp.sum(inputs * inputs, axis=-1, keepdims=True)) + 1e-06)

def short_conv(raw_rows, weight):
    kernel_len = weight.shape[0]
    length = raw_rows.shape[1]
    padded = jnp.pad(raw_rows, ((0, 0), (kernel_len - 1, 0), (0, 0)))
    total = padded[:, 0:length] * weight[0]
    for offset in range(1, kernel_len):
        total = total + padded[:, offset:offset + length] * weight[offset]
    return jax.nn.silu(total)

def unit_inverse(coupling, block_len):
    identity = jnp.eye(block_len, dtype=coupling.dtype)
    result = identity - coupling
    power = coupling
    span = 2
    while span < block_len:
        power = matmul_high(power, power)
        result = matmul_high(result, identity + power)
        span = span * 2
    return result

def to_blocks(array, block_len):
    seq_count, length, head_count = (array.shape[0], array.shape[1], array.shape[2])
    shaped = array.reshape(seq_count, length // block_len, block_len, head_count, -1)
    return jnp.moveaxis(shaped, 3, 1)

def delta_rule(queries, key_rows, values, decays, beta_rates, block_len):
    seq_count, length, head_count, key_dim = queries.shape
    q_blocks = to_blocks(queries, block_len)
    k_blocks = to_blocks(key_rows, block_len)
    v_blocks = to_blocks(values, block_len)
    cumulative = jnp.cumsum(to_blocks(decays[..., None], block_len)[..., 0], axis=-1)
    beta_blocks = to_blocks(beta_rates[..., None], block_len)[..., 0]
    positions = jnp.arange(block_len)
    causal = positions[:, None] >= positions[None, :]
    strict = positions[:, None] > positions[None, :]
    gaps = jnp.where(causal, cumulative[..., :, None] - cumulative[..., None, :], 0.0)
    fading = jnp.where(causal, jnp.exp(gaps), 0.0)
    key_key = jnp.einsum('...id,...jd->...ij', k_blocks, k_blocks, precision=HIGH)
    coupling = jnp.where(strict, beta_blocks[..., :, None] * fading * key_key, 0.0)
    inverse = unit_inverse(coupling, block_len)
    targets = jnp.concatenate([(beta_blocks * jnp.exp(cumulative))[..., None] * k_blocks, beta_blocks[..., None] * v_blocks], axis=-1)
    solved = matmul_high(inverse, targets)
    key_part = solved[..., :key_dim]
    value_part = solved[..., key_dim:]
    query_key = jnp.einsum('...id,...jd->...ij', q_blocks, k_blocks, precision=HIGH) * fading
    query_fade = q_blocks * jnp.exp(cumulative)[..., None]
    key_fade = k_blocks * jnp.exp(cumulative[..., -1:] - cumulative)[..., None]
    block_fade = jnp.exp(cumulative[..., -1])
    sequence = tuple((jnp.moveaxis(member, 2, 0) for member in (key_part, value_part, query_fade, key_fade, query_key, block_fade)))

    def advance(state, block):
        key_now, value_now, query_now, fade_now, scores_now, decay_now = block
        fresh = value_now - matmul_high(key_now, state)
        output = matmul_high(query_now, state) + matmul_high(scores_now, fresh)
        state = decay_now[..., None, None] * state + jnp.einsum('...ck,...cv->...kv', fade_now, fresh, precision=HIGH)
        return (state, output)
    start = jnp.zeros((seq_count, head_count, key_dim, values.shape[-1]), jnp.float32)
    final_state, outputs = lax.scan(jax.checkpoint(advance), start, sequence)
    return jnp.transpose(outputs, (1, 0, 3, 2, 4)).reshape(seq_count, length, head_count, -1)

def local_mixer(query_raw, key_raw, value_raw, gate_raw, alpha_raw, beta_raw, conv_query, conv_key, conv_value, decay_log, decay_bias, onorm_gain, seq_count, head_count):
    row_count = query_raw.shape[0]
    length = row_count // seq_count

    def conv_heads(raw_rows, weight):
        return short_conv(raw_rows.reshape(seq_count, length, -1), weight).reshape(seq_count, length, head_count, -1)
    queries = unit_rows(conv_heads(query_raw, conv_query))
    queries = queries * queries.shape[-1] ** (-0.5)
    key_rows = unit_rows(conv_heads(key_raw, conv_key))
    values = conv_heads(value_raw, conv_value)
    beta_rates = jax.nn.sigmoid(beta_raw).reshape(seq_count, length, head_count)
    decays = (-jnp.exp(decay_log) * jax.nn.softplus(alpha_raw + decay_bias)).reshape(seq_count, length, head_count)
    mixed = delta_rule(queries, key_rows, values, decays, beta_rates, STRETCH)
    gates = gate_raw.reshape(seq_count, length, head_count, -1)
    normed = mixed * lax.rsqrt(lax.optimization_barrier(jnp.mean(mixed * mixed, axis=-1, keepdims=True)) + EPS_NORM) * onorm_gain * jax.nn.silu(gates)
    return normed.reshape(row_count, -1)

def forward(tokens_f, norm1_gain, norm2_gain, query_weight, key_weight, value_weight, outgate_weight, alpha_weight, beta_weight, conv_query, conv_key, conv_value, decay_log, decay_bias, onorm_gain, output_weight, gate_weight, up_weight, down_weight, seq_count):
    hidden_one = low(norm_one(tokens_f, norm1_gain))

    def project(weight):
        return low_back(jnp.dot(hidden_one, weight, precision=HIGH))
    normed = local_mixer(project(query_weight), project(key_weight), project(value_weight), project(outgate_weight), project(alpha_weight), project(beta_weight), conv_query, conv_key, conv_value, decay_log, decay_bias, onorm_gain, seq_count, HEADS)
    mixer_out = low_back(jnp.dot(low(normed), output_weight, precision=HIGH))
    middle = tokens_f + mixer_out
    hidden_two = low(norm_one(middle, norm2_gain))
    gate = low_back(jnp.dot(hidden_two, gate_weight, precision=HIGH))
    upward = low_back(jnp.dot(hidden_two, up_weight, precision=HIGH))
    active = low(jax.nn.silu(gate) * upward)
    return middle + jnp.dot(active, down_weight, precision=HIGH)

def reference(tokens, cotangent, norm1_gain, norm2_gain, query_weight, key_weight, value_weight, outgate_weight, alpha_weight, beta_weight, conv_query, conv_key, conv_value, decay_log, decay_bias, onorm_gain, output_weight, gate_weight, up_weight, down_weight):
    params = tuple((member.astype(jnp.float32) for member in (norm1_gain, norm2_gain, query_weight, key_weight, value_weight, outgate_weight, alpha_weight, beta_weight, conv_query, conv_key, conv_value, decay_log, decay_bias, onorm_gain, output_weight, gate_weight, up_weight, down_weight)))
    total_seqs = TOKENS // SEQ
    group = math.gcd(total_seqs, max(1, 4096 // SEQ))
    step_count = total_seqs // group
    group_rows = group * SEQ
    token_blocks = tokens.reshape(step_count, group_rows, D)
    cot_blocks = cotangent.reshape(step_count, group_rows, D)

    def apply(tokens_f, *weights):
        return forward(tokens_f, *weights, group)

    def advance(totals, blocks):
        block_tokens, block_cot = blocks
        result, back = jax.vjp(apply, block_tokens.astype(jnp.float32), *params)
        grads = back(block_cot.astype(jnp.float32))
        totals = tuple((first + second for first, second in zip(totals, grads[1:])))
        return (totals, (result, grads[0]))
    start = tuple((jnp.zeros_like(member) for member in params))
    totals, (outputs, token_grads) = lax.scan(advance, start, (token_blocks, cot_blocks))
    block_output = outputs.reshape(TOKENS, D).astype(jnp.bfloat16)
    g_norm1, g_norm2, g_query, g_key, g_value, g_outgate, g_alpha, g_beta, g_convq, g_convk, g_convv, g_dlog, g_dbias, g_onorm, g_output, g_gate, g_up, g_down = totals
    return (block_output, token_grads.reshape(TOKENS, D), g_norm1, g_norm2, g_query, g_key, g_value, g_outgate, g_alpha, g_beta, g_convq, g_convk, g_convv, g_dlog, g_dbias, g_onorm, g_output, g_gate, g_up, g_down)
```

```python
import functools
import jax
import jax.numpy as jnp
from jax import lax
from jax.sharding import PartitionSpec as P
from jax.experimental import pallas as pl
from jax.experimental.pallas import tpu as pltpu

SEQ = 2048
BLOCK = 256
HALF = 128
EPS_NORM = 1e-05
EPS_UNIT = 1e-06
BF = jnp.bfloat16
F32 = jnp.float32
HIGH = lax.Precision.HIGHEST


def mm(left, right):
    return lax.dot_general(
        left.astype(BF), right.astype(BF), (((1,), (0,)), ((), ())), preferred_element_type=F32
    )


def mm_nt(left, right):
    return lax.dot_general(
        left.astype(BF), right.astype(BF), (((1,), (1,)), ((), ())), preferred_element_type=F32
    )


def mm_tn(left, right):
    return lax.dot_general(
        left.astype(BF), right.astype(BF), (((0,), (0,)), ((), ())), preferred_element_type=F32
    )


def mm_exact(left, right):
    return lax.dot_general(
        left, right, (((1,), (0,)), ((), ())), precision=HIGH, preferred_element_type=F32
    )


def iota2(rows, columns):
    return (
        lax.broadcasted_iota(jnp.int32, (rows, columns), 0),
        lax.broadcasted_iota(jnp.int32, (rows, columns), 1),
    )


def unit_lower_inverse(blocks):
    size = blocks[0].shape[0]
    row, col = iota2(size, size)
    eye = jnp.where(row == col, 1.0, 0.0).astype(F32)
    first = jnp.where((row ^ col) == 1, 1.0, 0.0).astype(F32)
    results = [eye - block * first for block in blocks]
    lows = [block.astype(BF) for block in blocks]
    shift = 1
    while (1 << shift) < size:
        mask = jnp.where(((row >> shift) ^ (col >> shift)) == 1, 1.0, 0.0).astype(BF)
        halves = [result.astype(BF) for result in results]
        inner = [mm(low * mask, half).astype(BF) for low, half in zip(lows, halves)]
        results = [
            result - mm(half, part) for result, half, part in zip(results, halves, inner)
        ]
        shift += 1
    return results


def softplus(value):
    return jnp.maximum(value, 0.0) + jnp.log1p(jnp.exp(-jnp.abs(value)))


def lower_ones(size):
    row, col = iota2(size, size)
    return jnp.where(row >= col, 1.0, 0.0).astype(F32)


def fades(total, total_t, index):
    row, col = iota2(BLOCK, BLOCK)
    gaps = total[:, index : index + 1] - total_t[index : index + 1, :]
    fading = jnp.exp(jnp.where(row >= col, gaps, -1e30))
    return fading, row > col


def forward_kernel(
    heads,
    per_seq,
    x_ref,
    gain_ref,
    w_ref,
    taps_ref,
    rate_ref,
    bias_ref,
    onorm_ref,
    hidden_ref,
    raw_ref,
    normed_ref,
    mixed_ref,
    state_ref,
    inv_ref,
    solved_ref,
    query_eff_ref,
    keyw_ref,
    carry_ref,
    ext_ref,
):
    key_dim = state_ref.shape[2]
    value_dim = state_ref.shape[3]
    qk = heads * key_dim
    conv_width = taps_ref.shape[1]
    gate_at = conv_width
    small_at = gate_at + heads * value_dim
    step = pl.program_id(0)

    @pl.when(step % per_seq == 0)
    def _():
        carry_ref[...] = jnp.zeros_like(carry_ref)
        ext_ref[0:8, :] = jnp.zeros((8, conv_width), F32)

    @pl.when(step % per_seq != 0)
    def _():
        ext_ref[0:8, :] = ext_ref[BLOCK : BLOCK + 8, :]

    inputs = x_ref[...].astype(F32)
    inverse = lax.rsqrt(jnp.mean(inputs * inputs, axis=-1, keepdims=True) + EPS_NORM)
    hidden = (inputs * inverse * gain_ref[...]).astype(BF)
    hidden_ref[...] = hidden
    ext_ref[8:, :] = mm(hidden, w_ref[:, :conv_width])
    raw_ref[:, :conv_width] = ext_ref[8:, :]
    raw_ref[:, gate_at:] = mm(hidden, w_ref[:, gate_at:])

    small = raw_ref[:, small_at:]
    betas = jax.nn.sigmoid(small)
    decays = -rate_ref[...] * softplus(small + bias_ref[...])
    total = mm_exact(lower_ones(BLOCK), decays)
    total_t = total.T

    def conv(start, width):
        acc = taps_ref[0:1, start : start + width] * ext_ref[pl.ds(5, BLOCK), start : start + width]
        for tap in range(1, 4):
            acc = acc + (
                taps_ref[tap : tap + 1, start : start + width]
                * ext_ref[pl.ds(5 + tap, BLOCK), start : start + width]
            )
        return acc * jax.nn.sigmoid(acc)

    def unit(value):
        return value * lax.rsqrt(jnp.sum(value * value, axis=-1, keepdims=True) + EPS_UNIT)

    parts = []
    for head in range(heads):
        query = unit(conv(head * key_dim, key_dim)) * key_dim ** (-0.5)
        keys = unit(conv(qk + head * key_dim, key_dim))
        values = conv(2 * qk + head * value_dim, value_dim)
        beta = betas[:, heads + head : heads + head + 1]
        fading, strict = fades(total, total_t, head)
        key_low = keys.astype(BF)
        coupling = jnp.where(strict, beta * fading * mm_nt(key_low, key_low), 0.0)
        scores = (mm_nt(query, key_low) * fading).astype(BF)
        parts.append((query, keys, values, beta, coupling, scores))
    blocks = []
    for part in parts:
        coupling = part[4]
        blocks += [coupling[:HALF, :HALF], coupling[HALF:, HALF:]]
    inverses = unit_lower_inverse(blocks)
    for head in range(heads):
        query, keys, values, beta, coupling, scores = parts[head]
        top, bottom = inverses[2 * head], inverses[2 * head + 1]
        cross = -mm(bottom, mm(coupling[HALF:, :HALF], top))
        inverse_low = jnp.concatenate(
            [
                jnp.concatenate([top.astype(BF), jnp.zeros((HALF, HALF), BF)], axis=1),
                jnp.concatenate([cross.astype(BF), bottom.astype(BF)], axis=1),
            ],
            axis=0,
        )
        inv_ref[0, head] = inverse_low
        column = total[:, head : head + 1]
        last = total[BLOCK - 1 :, head : head + 1]
        grown = jnp.exp(column)
        targets = jnp.concatenate(
            [(((beta * grown) * keys)).astype(BF), (beta * values).astype(BF)], axis=1
        )
        solved = mm(inverse_low, targets)
        solved_low = solved.astype(BF)
        solved_ref[0, head] = solved_low
        spread = mm(scores, solved_low)
        query_eff = (query * grown - spread[:, :key_dim]).astype(BF)
        query_eff_ref[0, head] = query_eff
        key_fade = keys * jnp.exp(last - column)
        gathered = mm_tn(key_fade, solved_low)
        keyw = gathered[:, :key_dim].astype(BF)
        keyw_ref[0, head] = keyw
        state = carry_ref[head]
        state_ref[0, head] = state
        state_low = state.astype(BF)
        mixed = mm(query_eff, state_low) + spread[:, key_dim:]
        carry_ref[head] = jnp.exp(last) * state - mm(keyw, state_low) + gathered[:, key_dim:]
        span = slice(head * value_dim, (head + 1) * value_dim)
        mixed_ref[:, span] = mixed
        gate = raw_ref[:, gate_at + head * value_dim : gate_at + (head + 1) * value_dim]
        scale = lax.rsqrt(jnp.mean(mixed * mixed, axis=-1, keepdims=True) + EPS_NORM)
        normed_ref[:, span] = (
            mixed * scale * onorm_ref[...] * (gate * jax.nn.sigmoid(gate))
        ).astype(BF)


def mixer_forward(tokens, gain, weights, taps, rate, bias, onorm, heads):
    rows, width = tokens.shape
    total_width = weights.shape[1]
    conv_width = taps.shape[1]
    value_dim = onorm.shape[1]
    value_all = heads * value_dim
    key_dim = (conv_width - value_all) // (2 * heads)
    steps = rows // BLOCK
    whole = lambda shape: pl.BlockSpec(shape, lambda i: (0,) * len(shape))
    rows_of = lambda columns: pl.BlockSpec((BLOCK, columns), lambda i: (i, 0))
    each = lambda a, b: pl.BlockSpec((1, heads, a, b), lambda i: (i, 0, 0, 0))
    shape = jax.ShapeDtypeStruct
    return pl.pallas_call(
        functools.partial(forward_kernel, heads, SEQ // BLOCK),
        grid=(steps,),
        in_specs=[
            rows_of(width),
            whole((1, width)),
            whole((width, total_width)),
            whole(taps.shape),
            whole(rate.shape),
            whole(bias.shape),
            whole(onorm.shape),
        ],
        out_specs=[
            rows_of(width),
            rows_of(total_width),
            rows_of(value_all),
            rows_of(value_all),
            each(key_dim, value_dim),
            each(BLOCK, BLOCK),
            each(BLOCK, key_dim + value_dim),
            each(BLOCK, key_dim),
            each(key_dim, key_dim),
        ],
        out_shape=[
            shape((rows, width), BF),
            shape((rows, total_width), F32),
            shape((rows, value_all), BF),
            shape((rows, value_all), F32),
            shape((steps, heads, key_dim, value_dim), F32),
            shape((steps, heads, BLOCK, BLOCK), BF),
            shape((steps, heads, BLOCK, key_dim + value_dim), BF),
            shape((steps, heads, BLOCK, key_dim), BF),
            shape((steps, heads, key_dim, key_dim), BF),
        ],
        scratch_shapes=[
            pltpu.VMEM((heads, key_dim, value_dim), F32),
            pltpu.VMEM((BLOCK + 8, conv_width), F32),
        ],
        compiler_params=pltpu.CompilerParams(
            dimension_semantics=("arbitrary",), vmem_limit_bytes=56 * 1024 * 1024
        ),
        name="mixer_forward",
    )(tokens, gain, weights, taps, rate, bias, onorm)


def backward_kernel(
    heads,
    per_seq,
    place_ref,
    dmix_ref,
    wout_ref,
    raw_ref,
    halo_ref,
    mixed_ref,
    state_ref,
    inv_ref,
    solved_ref,
    query_eff_ref,
    keyw_ref,
    taps_ref,
    rate_ref,
    bias_ref,
    onorm_ref,
    draw_ref,
    dtaps_ref,
    dsmall_ref,
    donorm_ref,
    carry_ref,
    ext_ref,
    dext_ref,
):
    key_dim = state_ref.shape[2]
    value_dim = state_ref.shape[3]
    qk = heads * key_dim
    conv_width = taps_ref.shape[1]
    gate_at = conv_width
    small_at = gate_at + heads * value_dim
    step = pl.program_id(0)
    block = pl.num_programs(0) - 1 - step

    @pl.when(step == 0)
    def _():
        dtaps_ref[...] = jnp.zeros_like(dtaps_ref)
        dsmall_ref[...] = jnp.zeros_like(dsmall_ref)
        donorm_ref[...] = jnp.zeros_like(donorm_ref)

    @pl.when(step % per_seq == 0)
    def _():
        carry_ref[...] = jnp.zeros_like(carry_ref)
        dext_ref[BLOCK:, :] = jnp.zeros((8, conv_width), F32)

    @pl.when(step % per_seq != 0)
    def _():
        dext_ref[BLOCK:, :] = dext_ref[0:8, :]

    keep = jnp.where(block % per_seq == 0, 0.0, 1.0)
    ext_ref[0:8, :] = halo_ref[:, :conv_width] * keep
    ext_ref[8:, :] = raw_ref[:, :conv_width]

    small = raw_ref[:, small_at:]
    betas = jax.nn.sigmoid(small)
    shifted = small + bias_ref[...]
    decays = -rate_ref[...] * softplus(shifted)
    lower = lower_ones(BLOCK)
    total = mm_exact(lower, decays)
    total_t = total.T
    lane = lax.broadcasted_iota(jnp.int32, (1, HALF), 1)
    ones = jnp.ones((1, BLOCK), F32)

    def conv(start, width):
        acc = taps_ref[0:1, start : start + width] * ext_ref[pl.ds(5, BLOCK), start : start + width]
        for tap in range(1, 4):
            acc = acc + (
                taps_ref[tap : tap + 1, start : start + width]
                * ext_ref[pl.ds(5 + tap, BLOCK), start : start + width]
            )
        sig = jax.nn.sigmoid(acc)
        return acc * sig, sig * (1.0 + acc * (1.0 - sig))

    def back_unit(value, scale, grad):
        along = jnp.sum(value * grad, axis=-1, keepdims=True)
        return scale * grad - value * (scale * scale * scale * along)

    def inv_norm(value):
        return lax.rsqrt(jnp.sum(value * value, axis=-1, keepdims=True) + EPS_UNIT)

    small_grad = jnp.zeros((BLOCK, HALF), F32)
    total_grad = jnp.zeros((BLOCK, HALF), F32)
    col_rows = []
    dnormed = mm(dmix_ref[...], wout_ref[...])
    for head in range(heads):
        span = slice(head * value_dim, (head + 1) * value_dim)
        gate = raw_ref[:, gate_at + head * value_dim : gate_at + (head + 1) * value_dim]
        sig = jax.nn.sigmoid(gate)
        silu = gate * sig
        mixed = mixed_ref[:, span]
        scale = lax.rsqrt(jnp.mean(mixed * mixed, axis=-1, keepdims=True) + EPS_NORM)
        unit_mixed = mixed * scale
        grad = dnormed[:, span]
        onorm = onorm_ref[...]
        grad_unit = grad * unit_mixed
        donorm_ref[...] += jnp.sum(grad_unit * silu, axis=0, keepdims=True)
        draw_ref[:, gate_at + head * value_dim : gate_at + (head + 1) * value_dim] = (
            grad_unit * onorm * (sig * (1.0 + gate * (1.0 - sig)))
        ).astype(BF)
        grad_on = grad * onorm * silu
        along = jnp.mean(mixed * grad_on, axis=-1, keepdims=True)
        dmixed = scale * grad_on - mixed * (scale * scale * scale * along)
        dmixed_low = dmixed.astype(BF)

        query_pre, query_slope = conv(head * key_dim, key_dim)
        key_pre, key_slope = conv(qk + head * key_dim, key_dim)
        values, value_slope = conv(2 * qk + head * value_dim, value_dim)
        query_scale = inv_norm(query_pre)
        key_scale = inv_norm(key_pre)
        factor = key_dim ** (-0.5)
        query = query_pre * query_scale * factor
        keys = key_pre * key_scale
        beta = betas[:, heads + head : heads + head + 1]
        fading, strict = fades(total, total_t, head)
        query_low = query.astype(BF)
        key_low = keys.astype(BF)
        key_key = jnp.where(strict, mm_nt(key_low, key_low) * fading, 0.0)
        scores = mm_nt(query_low, key_low) * fading
        scores_low = scores.astype(BF)
        column = total[:, head : head + 1]
        last = total[BLOCK - 1 :, head : head + 1]
        grown = jnp.exp(column)
        rest = jnp.exp(last - column)
        key_fade = keys * rest
        key_fade_low = key_fade.astype(BF)

        state = state_ref[0, head]
        state_low = state.astype(BF)
        dstate = carry_ref[head]
        dstate_low = dstate.astype(BF)
        solved_low = solved_ref[0, head]
        key_part = solved_low[:, :key_dim]
        fresh = solved_low[:, key_dim:].astype(F32) - mm(key_part, state_low)
        fresh_low = fresh.astype(BF)
        dfresh = mm_tn(scores_low, dmixed_low) + mm(key_fade_low, dstate_low)
        dfresh_low = dfresh.astype(BF)
        carry_ref[head] = (
            jnp.exp(last) * dstate
            - mm_tn(keyw_ref[0, head], dstate_low)
            + mm_tn(query_eff_ref[0, head], dmixed_low)
        )
        dlast = jnp.exp(last) * jnp.sum(
            jnp.sum(state * dstate, axis=1, keepdims=True), axis=0, keepdims=True
        )
        dscores = mm_nt(dmixed_low, fresh_low)
        dquery_fade = mm_nt(dmixed_low, state_low)
        dkey_fade = mm_nt(fresh_low, dstate_low)
        dkey_part = -mm_nt(dfresh_low, state_low)
        dsolved = jnp.concatenate([dkey_part.astype(BF), dfresh_low], axis=1)
        dtargets = mm_tn(inv_ref[0, head], dsolved)
        dcoupling = -mm_nt(dtargets, solved_low)
        dkey_target = dtargets[:, :key_dim]
        dvalue_target = dtargets[:, key_dim:]

        pair = dcoupling * key_key
        dfade = beta * pair + dscores * scores
        dpair = (jnp.where(strict, dcoupling * (beta * fading), 0.0)).astype(BF)
        dquery_key = (dscores * fading).astype(BF)
        dquery = dquery_fade * grown + mm(dquery_key, key_low)
        fade_rows = jnp.sum(dkey_fade * key_fade, axis=-1, keepdims=True)
        grown_key = grown * keys
        target_rows = jnp.sum(dkey_target * grown_key, axis=-1, keepdims=True)
        dkeys = (
            dkey_fade * rest
            + dkey_target * (beta * grown)
            + mm(dpair, key_low)
            + mm_tn(dpair, key_low)
            + mm_tn(dquery_key, query_low)
        )
        dvalues = dvalue_target * beta
        dbeta = (
            jnp.sum(pair, axis=-1, keepdims=True)
            + target_rows
            + jnp.sum(dvalue_target * values, axis=-1, keepdims=True)
        )
        row_part = (
            jnp.sum(dfade, axis=-1, keepdims=True)
            + beta * target_rows
            + jnp.sum(dquery_fade * query, axis=-1, keepdims=True) * grown
            - fade_rows
        )
        dlast = dlast + jnp.sum(fade_rows, axis=0, keepdims=True)
        place = lax.broadcasted_iota(jnp.int32, (BLOCK, 1), 0)
        row_part = row_part + jnp.where(place == BLOCK - 1, dlast, 0.0)
        col_rows.append(jnp.sum(dfade, axis=0, keepdims=True))
        total_grad = total_grad + jnp.where(lane == head, row_part, 0.0)
        small_grad = small_grad + jnp.where(lane == heads + head, dbeta, 0.0)

        dquery_pre = back_unit(query_pre, query_scale, dquery * factor) * query_slope
        dkey_pre = back_unit(key_pre, key_scale, dkeys) * key_slope
        dext_ref[0:BLOCK, head * key_dim : (head + 1) * key_dim] = dquery_pre
        dext_ref[0:BLOCK, qk + head * key_dim : qk + (head + 1) * key_dim] = dkey_pre
        dext_ref[
            0:BLOCK, 2 * qk + head * value_dim : 2 * qk + (head + 1) * value_dim
        ] = dvalues * value_slope

    filler = jnp.zeros((HALF - heads, BLOCK), F32)
    total_grad = total_grad - jnp.concatenate(col_rows + [filler], axis=0).T
    row, col = iota2(BLOCK, BLOCK)
    upper = jnp.where(row <= col, 1.0, 0.0).astype(F32)
    ddecay = mm_exact(upper, total_grad)
    dalpha = ddecay * (-rate_ref[...]) * jax.nn.sigmoid(shifted)
    dsmall_ref[0:1, :] += jnp.sum(ddecay * decays, axis=0, keepdims=True)
    dsmall_ref[1:2, :] += jnp.sum(dalpha, axis=0, keepdims=True)
    draw_ref[:, small_at:] = (
        jnp.where(lane < heads, dalpha, small_grad * betas * (1.0 - betas))
    ).astype(BF)

    width = HALF
    for start in range(0, conv_width, width):
        span = slice(start, start + width)
        grad = dext_ref[0:BLOCK, span]
        acc = taps_ref[3:4, span] * grad
        for tap in range(3):
            acc = acc + taps_ref[tap : tap + 1, span] * dext_ref[pl.ds(3 - tap, BLOCK), span]
        draw_ref[:, span] = acc.astype(BF)
        for tap in range(4):
            dtaps_ref[tap : tap + 1, span] += jnp.sum(
                grad * ext_ref[pl.ds(5 + tap, BLOCK), span], axis=0, keepdims=True
            )


def mixer_backward(place, part_rows, dmix, wout_t, saved, taps, rate, bias, onorm, heads):
    raw, mixed, states, inverses, solved, query_eff, keyw = saved
    rows, width = dmix.shape
    total_width = raw.shape[1]
    conv_width = taps.shape[1]
    value_dim = onorm.shape[1]
    value_all = heads * value_dim
    key_dim = (conv_width - value_all) // (2 * heads)
    steps = rows // BLOCK
    last = steps - 1
    whole = lambda shape: pl.BlockSpec(shape, lambda i, p: (0,) * len(shape))
    rows_of = lambda columns: pl.BlockSpec((BLOCK, columns), lambda i, p: (last - i, 0))
    each = lambda a, b: pl.BlockSpec((1, heads, a, b), lambda i, p: (last - i, 0, 0, 0))
    shape = jax.ShapeDtypeStruct
    halo = pl.BlockSpec(
        (8, total_width), lambda i, p: (jnp.maximum((last - i) * (BLOCK // 8) - 1, 0), 0)
    )
    per = part_rows // BLOCK

    def mixed_order(i, place_ref):
        block = last - i
        return (((block // per) ^ place_ref[0]) * per + block % per, 0)

    return pl.pallas_call(
        functools.partial(backward_kernel, heads, SEQ // BLOCK),
        grid_spec=pltpu.PrefetchScalarGridSpec(
        num_scalar_prefetch=1,
        grid=(steps,),
        in_specs=[
            pl.BlockSpec((BLOCK, width), mixed_order),
            whole(wout_t.shape),
            rows_of(total_width),
            halo,
            rows_of(value_all),
            each(key_dim, value_dim),
            each(BLOCK, BLOCK),
            each(BLOCK, key_dim + value_dim),
            each(BLOCK, key_dim),
            each(key_dim, key_dim),
            whole(taps.shape),
            whole(rate.shape),
            whole(bias.shape),
            whole(onorm.shape),
        ],
        out_specs=[
            rows_of(total_width),
            whole((8, conv_width)),
            whole((8, HALF)),
            whole((1, value_dim)),
        ],
        scratch_shapes=[
            pltpu.VMEM((heads, key_dim, value_dim), F32),
            pltpu.VMEM((BLOCK + 8, conv_width), F32),
            pltpu.VMEM((BLOCK + 8, conv_width), F32),
        ],
        ),
        out_shape=[
            shape((rows, total_width), BF),
            shape((8, conv_width), F32),
            shape((8, HALF), F32),
            shape((1, value_dim), F32),
        ],
        compiler_params=pltpu.CompilerParams(
            dimension_semantics=("arbitrary",), vmem_limit_bytes=56 * 1024 * 1024
        ),
        name="mixer_backward",
    )(
        place, dmix, wout_t, raw, raw, mixed, states, inverses, solved, query_eff, keyw,
        taps, rate, bias, onorm,
    )


def dot_plain(left_side, right_side):
    return jnp.dot(left_side, right_side, preferred_element_type=F32)


def dot_right_t(left_side, right_side):
    return lax.dot_general(
        left_side, right_side, (((1,), (1,)), ((), ())), preferred_element_type=F32
    )


def dot_left_t(left_side, right_side):
    return lax.dot_general(
        left_side, right_side, (((0,), (0,)), ((), ())), preferred_element_type=F32
    )


def swap(value, flip):
    count = lax.axis_size("tensor")
    return lax.ppermute(value, "tensor", [(i, i ^ flip) for i in range(count)])


def gather_blocks(block):
    far = swap(block, 2)
    near = swap(block, 1)
    return [block, near, far, swap(far, 1)]


def scatter_sum(parts):
    far = parts[2].astype(F32) + swap(parts[3].astype(BF), 1).astype(F32)
    far = swap(far.astype(BF), 2).astype(F32)
    near = parts[0].astype(F32) + swap(parts[1].astype(BF), 1).astype(F32)
    return near + far


def pad_columns(value, width):
    return jnp.pad(value, ((0, 0), (0, width - value.shape[1])))


def round_up(value, unit):
    return -(-value // unit) * unit


def sum_dp(value):
    return lax.psum_scatter(value.astype(BF), "dp", scatter_dimension=0, tiled=True).astype(F32)


def per_device(
    tokens,
    cotangent,
    norm1_gain,
    norm2_gain,
    query_weight,
    key_weight,
    value_weight,
    outgate_weight,
    alpha_weight,
    beta_weight,
    conv_query,
    conv_key,
    conv_value,
    decay_log,
    decay_bias,
    onorm_gain,
    output_weight,
    gate_weight,
    up_weight,
    down_weight,
):
    me = lax.axis_index("tensor")
    tensor_count = lax.axis_size("tensor")
    part_rows = cotangent.shape[0]
    width = tokens.shape[1]
    heads = alpha_weight.shape[1]
    units = gate_weight.shape[1]
    padded = round_up(units, 256)
    query_cols = query_weight.shape[1]
    value_cols = value_weight.shape[1]
    conv_width = 2 * query_cols + value_cols
    value_dim = onorm_gain.shape[0]

    small = pad_columns(jnp.concatenate([alpha_weight, beta_weight], axis=1), HALF)
    w_first = lax.all_gather(
        jnp.concatenate([query_weight, key_weight, value_weight, outgate_weight, small], axis=1),
        "dp",
        axis=0,
        tiled=True,
    )
    w_second = lax.all_gather(
        jnp.concatenate(
            [
                output_weight.T,
                pad_columns(gate_weight, padded),
                pad_columns(up_weight, padded),
                pad_columns(down_weight.T, padded),
            ],
            axis=1,
        ),
        "dp",
        axis=0,
        tiled=True,
    )
    w_out_t = w_second[:, :value_cols]
    w_pair = w_second[:, value_cols : value_cols + 2 * padded]
    w_down_t = w_second[:, value_cols + 2 * padded :]

    taps = jnp.concatenate([conv_query, conv_key, conv_value], axis=1)
    rate = pad_columns(jnp.exp(decay_log)[None], HALF)
    bias = pad_columns(decay_bias[None], HALF)
    onorm = onorm_gain[None]
    hidden_one, raw, normed, *saved = mixer_forward(
        tokens, norm1_gain[None], w_first, taps, rate, bias, onorm, heads
    )

    def block_of(value, flip):
        return lax.dynamic_slice_in_dim(value, (me ^ flip) * part_rows, part_rows, 0)

    normed_blocks = [block_of(normed, flip) for flip in range(4)]
    mixer_rows = scatter_sum([dot_right_t(block, w_out_t) for block in normed_blocks])
    inputs = block_of(tokens, 0).astype(F32)
    middle = inputs + mixer_rows
    inverse_two = lax.rsqrt(jnp.mean(middle * middle, axis=-1, keepdims=True) + EPS_NORM)
    unit_two = middle * inverse_two
    hidden_two = jnp.concatenate(gather_blocks((unit_two * norm2_gain).astype(BF)), axis=0)
    cot_all = jnp.concatenate(gather_blocks(cotangent), axis=0)
    pair = dot_plain(hidden_two, w_pair)
    gate, upward = pair[:, :padded], pair[:, padded:]
    sig = jax.nn.sigmoid(gate)
    silu = gate * sig
    active = (silu * upward).astype(BF)
    branch = dot_right_t(active, w_down_t).astype(BF)
    branch_rows = scatter_sum(
        [branch[part_rows * flip : part_rows * (flip + 1)] for flip in range(4)]
    )
    block_output = (middle + branch_rows).astype(BF)
    active_grad = dot_plain(cot_all, w_down_t)
    pair_grad = jnp.concatenate(
        [
            (active_grad * upward * (sig * (1.0 + gate * (1.0 - sig)))).astype(BF),
            (active_grad * silu).astype(BF),
        ],
        axis=1,
    )
    hidden_two_part = dot_right_t(pair_grad, w_pair).astype(BF)
    hidden_two_grad = scatter_sum(
        [hidden_two_part[part_rows * flip : part_rows * (flip + 1)] for flip in range(4)]
    )
    gain_two_part = jnp.sum(hidden_two_grad * unit_two, axis=0)
    gained_two = hidden_two_grad * norm2_gain
    middle_grad = (
        cotangent.astype(F32)
        + inverse_two * gained_two
        - unit_two * inverse_two * inverse_two * jnp.mean(middle * gained_two, axis=-1, keepdims=True)
    )
    middle_low = jnp.concatenate(gather_blocks(middle_grad.astype(BF)), axis=0)
    ffn_total = sum_dp(
        jnp.concatenate(
            [
                dot_left_t(hidden_two, pair_grad).astype(BF),
                dot_left_t(cot_all, active).astype(BF),
            ],
            axis=1,
        )
    )
    draw, dtaps, dsmall, donorm = mixer_backward(
        me[None].astype(jnp.int32),
        part_rows,
        middle_low,
        w_out_t,
        (raw,) + tuple(saved),
        taps,
        rate,
        bias,
        onorm,
        heads,
    )
    normed_mixed = jnp.concatenate(normed_blocks, axis=0)
    output_total = sum_dp(dot_left_t(middle_low, normed_mixed))
    hidden_one_grad = scatter_sum(
        [dot_right_t(block_of(draw, flip), w_first) for flip in range(4)]
    )
    proj_total = sum_dp(dot_left_t(hidden_one, draw))

    inverse_one = lax.rsqrt(jnp.mean(inputs * inputs, axis=-1, keepdims=True) + EPS_NORM)
    unit_one = inputs * inverse_one
    gain_one_part = jnp.sum(hidden_one_grad * unit_one, axis=0)
    gained = hidden_one_grad * norm1_gain
    tokens_grad = (
        middle_grad
        + inverse_one * gained
        - unit_one * inverse_one * inverse_one * jnp.mean(inputs * gained, axis=-1, keepdims=True)
    )

    tap_count = taps.shape[0]
    tap_width = max(conv_width, width)
    own_rows = jnp.concatenate(
        [pad_columns(dtaps[:tap_count], tap_width), pad_columns(dsmall[:2], tap_width)], axis=0
    )
    own_count = tap_count + 2
    shared_rows = jnp.stack(
        [
            jnp.pad(gain_one_part, (0, tap_width - width)),
            jnp.pad(gain_two_part, (0, tap_width - width)),
            jnp.pad(donorm[0], (0, tap_width - value_dim)),
        ]
    )
    table = jnp.concatenate(
        [
            lax.dynamic_update_slice_in_dim(
                jnp.zeros((own_count * tensor_count, tap_width), F32), own_rows, own_count * me, 0
            ),
            shared_rows,
        ],
        axis=0,
    )
    table = lax.psum(table, ("dp", "tensor"))
    own_total = lax.dynamic_slice_in_dim(table, own_count * me, own_count, 0)
    shared = table[own_count * tensor_count :]
    gain_share = width // tensor_count
    onorm_share = value_dim // tensor_count
    at = 2 * query_cols
    small_at = conv_width + value_cols
    return (
        block_output,
        tokens_grad,
        lax.dynamic_slice_in_dim(shared[0], me * gain_share, gain_share, 0),
        lax.dynamic_slice_in_dim(shared[1], me * gain_share, gain_share, 0),
        proj_total[:, :query_cols],
        proj_total[:, query_cols:at],
        proj_total[:, at:conv_width],
        proj_total[:, conv_width:small_at],
        proj_total[:, small_at : small_at + heads],
        proj_total[:, small_at + heads : small_at + 2 * heads],
        own_total[:tap_count, :query_cols],
        own_total[:tap_count, query_cols:at],
        own_total[:tap_count, at:conv_width],
        own_total[tap_count, :heads],
        own_total[tap_count + 1, :heads],
        lax.dynamic_slice_in_dim(shared[2], me * onorm_share, onorm_share, 0),
        output_total.T,
        ffn_total[:, :units],
        ffn_total[:, padded : padded + units],
        ffn_total[:, 2 * padded : 2 * padded + units].T,
    )


def solution(mesh):
    return jax.shard_map(
        per_device,
        mesh=mesh,
        in_specs=(
            P("dp", None),
            P(("dp", "tensor"), None),
            P(),
            P(),
            P("dp", "tensor"),
            P("dp", "tensor"),
            P("dp", "tensor"),
            P("dp", "tensor"),
            P("dp", "tensor"),
            P("dp", "tensor"),
            P(None, "tensor"),
            P(None, "tensor"),
            P(None, "tensor"),
            P("tensor"),
            P("tensor"),
            P(),
            P("tensor", "dp"),
            P("dp", "tensor"),
            P("dp", "tensor"),
            P("tensor", "dp"),
        ),
        out_specs=(
            P(("dp", "tensor"), None),
            P(("dp", "tensor"), None),
            P("tensor"),
            P("tensor"),
            P("dp", "tensor"),
            P("dp", "tensor"),
            P("dp", "tensor"),
            P("dp", "tensor"),
            P("dp", "tensor"),
            P("dp", "tensor"),
            P(None, "tensor"),
            P(None, "tensor"),
            P(None, "tensor"),
            P("tensor"),
            P("tensor"),
            P("tensor"),
            P("tensor", "dp"),
            P("dp", "tensor"),
            P("dp", "tensor"),
            P("tensor", "dp"),
        ),
        check_vma=False,
    )
```

```python
import functools
import jax
import jax.numpy as jnp
from jax import lax
from jax.sharding import PartitionSpec as P
from jax.experimental import pallas as pl
from jax.experimental.pallas import tpu as pltpu

SEQ = 2048
BLOCK = 256
HALF = 128
EPS_NORM = 1e-05
EPS_UNIT = 1e-06
BF = jnp.bfloat16
F32 = jnp.float32
HIGH = lax.Precision.HIGHEST


def mm(left, right):
    return lax.dot_general(
        left.astype(BF), right.astype(BF), (((1,), (0,)), ((), ())), preferred_element_type=F32
    )


def mm_nt(left, right):
    return lax.dot_general(
        left.astype(BF), right.astype(BF), (((1,), (1,)), ((), ())), preferred_element_type=F32
    )


def mm_tn(left, right):
    return lax.dot_general(
        left.astype(BF), right.astype(BF), (((0,), (0,)), ((), ())), preferred_element_type=F32
    )


def mm_exact(left, right):
    return lax.dot_general(
        left, right, (((1,), (0,)), ((), ())), precision=HIGH, preferred_element_type=F32
    )


def iota2(rows, columns):
    return (
        lax.broadcasted_iota(jnp.int32, (rows, columns), 0),
        lax.broadcasted_iota(jnp.int32, (rows, columns), 1),
    )


def unit_lower_inverse(blocks):
    size = blocks[0].shape[0]
    row, col = iota2(size, size)
    eye = jnp.where(row == col, 1.0, 0.0).astype(F32)
    first = jnp.where((row ^ col) == 1, 1.0, 0.0).astype(F32)
    results = [eye - block * first for block in blocks]
    lows = [block.astype(BF) for block in blocks]
    shift = 1
    while (1 << shift) < size:
        mask = jnp.where(((row >> shift) ^ (col >> shift)) == 1, 1.0, 0.0).astype(BF)
        halves = [result.astype(BF) for result in results]
        inner = [mm(low * mask, half).astype(BF) for low, half in zip(lows, halves)]
        results = [
            result - mm(half, part) for result, half, part in zip(results, halves, inner)
        ]
        shift += 1
    return results


def softplus(value):
    return jnp.maximum(value, 0.0) + jnp.log1p(jnp.exp(-jnp.abs(value)))


def lower_ones(size):
    row, col = iota2(size, size)
    return jnp.where(row >= col, 1.0, 0.0).astype(F32)


def fades(total, total_t, index):
    row, col = iota2(BLOCK, BLOCK)
    gaps = total[:, index : index + 1] - total_t[index : index + 1, :]
    fading = jnp.exp(jnp.where(row >= col, gaps, -1e30))
    return fading, row > col


def forward_kernel(
    heads,
    per_seq,
    pieces,
    place_ref,
    x_ref,
    gain_ref,
    taps_ref,
    rate_ref,
    bias_ref,
    *refs,
):
    (
        w_ref,
        hidden_ref,
        raw_ref,
        mixed_ref,
        state_ref,
        inv_ref,
        solved_ref,
        query_eff_ref,
        keyw_ref,
        carry_ref,
        ext_ref,
    ) = refs[pieces:]
    key_dim = state_ref.shape[2]
    value_dim = state_ref.shape[3]
    conv_width = taps_ref.shape[1]
    head_width = conv_width // heads
    step = pl.program_id(0)

    @pl.when(step == 0)
    def _():
        rows = w_ref.shape[0] // pieces
        for index in range(pieces):
            start = pl.multiple_of((place_ref[0] ^ index) * rows, rows)
            w_ref[pl.ds(start, rows), :] = refs[index][...]

    @pl.when(step % per_seq == 0)
    def _():
        carry_ref[...] = jnp.zeros_like(carry_ref)
        ext_ref[0:8, :] = jnp.zeros((8, conv_width), F32)

    @pl.when(step % per_seq != 0)
    def _():
        ext_ref[0:8, :] = ext_ref[BLOCK : BLOCK + 8, :]

    inputs = x_ref[...].astype(F32)
    inverse = lax.rsqrt(jnp.mean(inputs * inputs, axis=-1, keepdims=True) + EPS_NORM)
    hidden = (inputs * inverse * gain_ref[...]).astype(BF)
    hidden_ref[...] = hidden
    ext_ref[8:, :] = mm(hidden, w_ref[:, :conv_width])
    raw_ref[:, :conv_width] = ext_ref[8:, :]
    raw_ref[:, conv_width:] = mm(hidden, w_ref[:, conv_width:])

    small = raw_ref[:, conv_width:]
    betas = jax.nn.sigmoid(small)
    decays = -rate_ref[...] * softplus(small + bias_ref[...])
    total = mm_exact(lower_ones(BLOCK), decays)
    total_t = total.T

    def conv(start, width):
        acc = taps_ref[0:1, start : start + width] * ext_ref[pl.ds(5, BLOCK), start : start + width]
        for tap in range(1, 4):
            acc = acc + (
                taps_ref[tap : tap + 1, start : start + width]
                * ext_ref[pl.ds(5 + tap, BLOCK), start : start + width]
            )
        return acc * jax.nn.sigmoid(acc)

    def unit(value):
        return value * lax.rsqrt(jnp.sum(value * value, axis=-1, keepdims=True) + EPS_UNIT)

    parts = []
    for head in range(heads):
        start = head * head_width
        query = unit(conv(start, key_dim)) * key_dim ** (-0.5)
        keys = unit(conv(start + key_dim, key_dim))
        values = conv(start + 2 * key_dim, value_dim)
        beta = betas[:, heads + head : heads + head + 1]
        fading, strict = fades(total, total_t, head)
        key_low = keys.astype(BF)
        coupling = jnp.where(strict, beta * fading * mm_nt(key_low, key_low), 0.0)
        scores = (mm_nt(query, key_low) * fading).astype(BF)
        parts.append((query, keys, values, beta, coupling, scores))
    blocks = []
    for part in parts:
        coupling = part[4]
        blocks += [coupling[:HALF, :HALF], coupling[HALF:, HALF:]]
    inverses = unit_lower_inverse(blocks)
    for head in range(heads):
        query, keys, values, beta, coupling, scores = parts[head]
        top, bottom = inverses[2 * head], inverses[2 * head + 1]
        cross = -mm(bottom, mm(coupling[HALF:, :HALF], top))
        inverse_low = jnp.concatenate(
            [
                jnp.concatenate([top.astype(BF), jnp.zeros((HALF, HALF), BF)], axis=1),
                jnp.concatenate([cross.astype(BF), bottom.astype(BF)], axis=1),
            ],
            axis=0,
        )
        inv_ref[0, head] = inverse_low
        column = total[:, head : head + 1]
        last = total[BLOCK - 1 :, head : head + 1]
        grown = jnp.exp(column)
        targets = jnp.concatenate(
            [(((beta * grown) * keys)).astype(BF), (beta * values).astype(BF)], axis=1
        )
        solved = mm(inverse_low, targets)
        solved_low = solved.astype(BF)
        solved_ref[0, head] = solved_low
        spread = mm(scores, solved_low)
        query_eff = (query * grown - spread[:, :key_dim]).astype(BF)
        query_eff_ref[0, head] = query_eff
        key_fade = keys * jnp.exp(last - column)
        gathered = mm_tn(key_fade, solved_low)
        keyw = gathered[:, :key_dim].astype(BF)
        keyw_ref[0, head] = keyw
        state = carry_ref[head]
        state_ref[0, head] = state
        state_low = state.astype(BF)
        mixed = mm(query_eff, state_low) + spread[:, key_dim:]
        carry_ref[head] = jnp.exp(last) * state - mm(keyw, state_low) + gathered[:, key_dim:]
        mixed_ref[:, head * value_dim : (head + 1) * value_dim] = mixed


def mixer_forward(tokens, gain, pieces, place, taps, rate, bias, heads, value_dim):
    rows, width = tokens.shape
    total_width = pieces[0].shape[1]
    conv_width = taps.shape[1]
    value_all = heads * value_dim
    key_dim = (conv_width - value_all) // (2 * heads)
    steps = rows // BLOCK
    whole = lambda shape: pl.BlockSpec(shape, lambda i, p: (0,) * len(shape))
    rows_of = lambda columns: pl.BlockSpec((BLOCK, columns), lambda i, p: (i, 0))
    each = lambda a, b: pl.BlockSpec((1, heads, a, b), lambda i, p: (i, 0, 0, 0))
    shape = jax.ShapeDtypeStruct
    return pl.pallas_call(
        functools.partial(forward_kernel, heads, SEQ // BLOCK, len(pieces)),
        grid_spec=pltpu.PrefetchScalarGridSpec(
            num_scalar_prefetch=1,
            grid=(steps,),
            in_specs=[
                rows_of(width),
                whole((1, width)),
                whole(taps.shape),
                whole(rate.shape),
                whole(bias.shape),
            ]
            + [whole(piece.shape) for piece in pieces],
            out_specs=[
                whole((width, total_width)),
                rows_of(width),
                rows_of(total_width),
                rows_of(value_all),
                each(key_dim, value_dim),
                each(BLOCK, BLOCK),
                each(BLOCK, key_dim + value_dim),
                each(BLOCK, key_dim),
                each(key_dim, key_dim),
            ],
            scratch_shapes=[
                pltpu.VMEM((heads, key_dim, value_dim), F32),
                pltpu.VMEM((BLOCK + 8, conv_width), F32),
            ],
        ),
        out_shape=[
            shape((width, total_width), BF),
            shape((rows, width), BF),
            shape((rows, total_width), F32),
            shape((rows, value_all), F32),
            shape((steps, heads, key_dim, value_dim), F32),
            shape((steps, heads, BLOCK, BLOCK), BF),
            shape((steps, heads, BLOCK, key_dim + value_dim), BF),
            shape((steps, heads, BLOCK, key_dim), BF),
            shape((steps, heads, key_dim, key_dim), BF),
        ],
        compiler_params=pltpu.CompilerParams(
            dimension_semantics=("arbitrary",), vmem_limit_bytes=48 * 1024 * 1024
        ),
        cost_estimate=pl.CostEstimate(
            flops=rows * 20_000_000, bytes_accessed=rows * 60_000, transcendentals=0
        ),
        name="mixer_forward",
    )(place, tokens, gain, taps, rate, bias, *pieces)


def gated_kernel(
    heads,
    place_ref,
    hidden_ref,
    mixed_ref,
    wgate_ref,
    wout_ref,
    onorm_ref,
    *out_refs,
):
    value_dim = onorm_ref.shape[1]
    gates = mm(hidden_ref[...], wgate_ref[...])
    columns = []
    for head in range(heads):
        span = slice(head * value_dim, (head + 1) * value_dim)
        mixed = mixed_ref[:, span]
        gate = gates[:, span]
        scale = lax.rsqrt(jnp.mean(mixed * mixed, axis=-1, keepdims=True) + EPS_NORM)
        columns.append(
            (mixed * scale * onorm_ref[...] * (gate * jax.nn.sigmoid(gate))).astype(BF)
        )
    normed = jnp.concatenate(columns, axis=1)
    part = mm_nt(normed, wout_ref[...]).astype(BF)
    for index in range(2):

        @pl.when(pl.program_id(0) == index)
        def _():
            out_refs[index][...] = normed
            out_refs[2 + index][...] = part


def gated_out(place, first, part_rows, hidden, mixed, weights, onorm, heads):
    width = hidden.shape[1]
    value_all = mixed.shape[1]
    whole = lambda block, at: pl.BlockSpec(block, lambda i, p: (0, at))
    theirs = lambda columns: pl.BlockSpec(
        (part_rows, columns), lambda i, p: ((first - i) ^ p[0], 0)
    )
    shape = jax.ShapeDtypeStruct
    return pl.pallas_call(
        functools.partial(gated_kernel, heads),
        grid_spec=pltpu.PrefetchScalarGridSpec(
            num_scalar_prefetch=1,
            grid=(2,),
            in_specs=[
                theirs(width),
                theirs(value_all),
                whole((width, value_all), 0),
                whole((width, value_all), 1),
                whole(onorm.shape, 0),
            ],
            out_specs=[whole((part_rows, value_all), 0)] * 2 + [whole((part_rows, width), 0)] * 2,
        ),
        out_shape=[shape((part_rows, value_all), BF)] * 2 + [shape((part_rows, width), BF)] * 2,
        compiler_params=pltpu.CompilerParams(
            dimension_semantics=("arbitrary",), vmem_limit_bytes=48 * 1024 * 1024
        ),
        cost_estimate=pl.CostEstimate(
            flops=part_rows * 8_000_000, bytes_accessed=part_rows * 24_000, transcendentals=0
        ),
        name="gated_out",
    )(place, hidden, mixed, weights, weights, onorm)


def backward_kernel(
    heads,
    per_seq,
    place_ref,
    *all_refs,
):
    dmix_refs = all_refs[:4]
    (
    wout_ref,
    raw_ref,
    halo_ref,
    hidden_ref,
    wgate_ref,
    mixed_ref,
    state_ref,
    inv_ref,
    solved_ref,
    query_eff_ref,
    keyw_ref,
    taps_ref,
    rate_ref,
    bias_ref,
    onorm_ref,
    draw_ref,
    dtaps_ref,
    dsmall_ref,
    donorm_ref,
    carry_ref,
    ext_ref,
    dext_ref,
    dmix_ref,
    ) = all_refs[4:]
    key_dim = state_ref.shape[2]
    value_dim = state_ref.shape[3]
    conv_width = taps_ref.shape[1]
    head_width = conv_width // heads
    full_width = head_width + value_dim
    step = pl.program_id(0)
    block = pl.num_programs(0) - 1 - step

    per = dmix_refs[0].shape[0] // BLOCK
    source = (block // per) ^ place_ref[0]
    start = pl.multiple_of((block % per) * BLOCK, BLOCK)
    for index in range(4):

        @pl.when(source == index)
        def _():
            dmix_ref[...] = dmix_refs[index][pl.ds(start, BLOCK), :]

    @pl.when(step == 0)
    def _():
        dtaps_ref[...] = jnp.zeros_like(dtaps_ref)
        dsmall_ref[...] = jnp.zeros_like(dsmall_ref)
        donorm_ref[...] = jnp.zeros_like(donorm_ref)

    @pl.when(step % per_seq == 0)
    def _():
        carry_ref[...] = jnp.zeros_like(carry_ref)
        dext_ref[BLOCK:, :] = jnp.zeros((8, conv_width), F32)

    @pl.when(step % per_seq != 0)
    def _():
        dext_ref[BLOCK:, :] = dext_ref[0:8, :]

    keep = jnp.where(block % per_seq == 0, 0.0, 1.0)
    ext_ref[0:8, :] = halo_ref[...] * keep
    ext_ref[8:, :] = raw_ref[:, :conv_width]

    small = raw_ref[:, conv_width:]
    betas = jax.nn.sigmoid(small)
    shifted = small + bias_ref[...]
    decays = -rate_ref[...] * softplus(shifted)
    lower = lower_ones(BLOCK)
    total = mm_exact(lower, decays)
    total_t = total.T
    lane = lax.broadcasted_iota(jnp.int32, (1, HALF), 1)

    def conv(start, width):
        acc = taps_ref[0:1, start : start + width] * ext_ref[pl.ds(5, BLOCK), start : start + width]
        for tap in range(1, 4):
            acc = acc + (
                taps_ref[tap : tap + 1, start : start + width]
                * ext_ref[pl.ds(5 + tap, BLOCK), start : start + width]
            )
        sig = jax.nn.sigmoid(acc)
        return acc * sig, sig * (1.0 + acc * (1.0 - sig))

    def back_unit(value, scale, grad):
        along = jnp.sum(value * grad, axis=-1, keepdims=True)
        return scale * grad - value * (scale * scale * scale * along)

    def inv_norm(value):
        return lax.rsqrt(jnp.sum(value * value, axis=-1, keepdims=True) + EPS_UNIT)

    results = {}

    def head_work(head):
        span = slice(head * value_dim, (head + 1) * value_dim)
        at = head * head_width
        out_at = head * full_width
        grad = mm(dmix_ref[...], wout_ref[:, span])
        gate = mm(hidden_ref[...], wgate_ref[:, span])
        yield
        sig = jax.nn.sigmoid(gate)
        silu = gate * sig
        mixed = mixed_ref[:, span]
        scale = lax.rsqrt(jnp.mean(mixed * mixed, axis=-1, keepdims=True) + EPS_NORM)
        unit_mixed = mixed * scale
        onorm = onorm_ref[...]
        grad_unit = grad * unit_mixed
        donorm_ref[...] += jnp.sum(grad_unit * silu, axis=0, keepdims=True)
        draw_ref[:, out_at + head_width : out_at + full_width] = (
            grad_unit * onorm * (sig * (1.0 + gate * (1.0 - sig)))
        ).astype(BF)
        grad_on = grad * onorm * silu
        along = jnp.mean(mixed * grad_on, axis=-1, keepdims=True)
        dmixed = scale * grad_on - mixed * (scale * scale * scale * along)
        dmixed_low = dmixed.astype(BF)
        yield

        query_pre, query_slope = conv(at, key_dim)
        key_pre, key_slope = conv(at + key_dim, key_dim)
        values, value_slope = conv(at + 2 * key_dim, value_dim)
        query_scale = inv_norm(query_pre)
        key_scale = inv_norm(key_pre)
        factor = key_dim ** (-0.5)
        query = query_pre * query_scale * factor
        keys = key_pre * key_scale
        beta = betas[:, heads + head : heads + head + 1]
        fading, strict = fades(total, total_t, head)
        query_low = query.astype(BF)
        key_low = keys.astype(BF)
        key_key = jnp.where(strict, mm_nt(key_low, key_low) * fading, 0.0)
        scores = mm_nt(query_low, key_low) * fading
        scores_low = scores.astype(BF)
        column = total[:, head : head + 1]
        last = total[BLOCK - 1 :, head : head + 1]
        grown = jnp.exp(column)
        rest = jnp.exp(last - column)
        key_fade = keys * rest
        key_fade_low = key_fade.astype(BF)
        yield

        state = state_ref[0, head]
        state_low = state.astype(BF)
        dstate = carry_ref[head]
        dstate_low = dstate.astype(BF)
        solved_low = solved_ref[0, head]
        key_part = solved_low[:, :key_dim]
        fresh = solved_low[:, key_dim:].astype(F32) - mm(key_part, state_low)
        fresh_low = fresh.astype(BF)
        yield
        dfresh = mm_tn(scores_low, dmixed_low) + mm(key_fade_low, dstate_low)
        dfresh_low = dfresh.astype(BF)
        yield
        carry_ref[head] = (
            jnp.exp(last) * dstate
            - mm_tn(keyw_ref[0, head], dstate_low)
            + mm_tn(query_eff_ref[0, head], dmixed_low)
        )
        dlast = jnp.exp(last) * jnp.sum(
            jnp.sum(state * dstate, axis=1, keepdims=True), axis=0, keepdims=True
        )
        yield
        dscores = mm_nt(dmixed_low, fresh_low)
        dquery_fade = mm_nt(dmixed_low, state_low)
        dkey_fade = mm_nt(fresh_low, dstate_low)
        dkey_part = -mm_nt(dfresh_low, state_low)
        yield
        dsolved = jnp.concatenate([dkey_part.astype(BF), dfresh_low], axis=1)
        dtargets = mm_tn(inv_ref[0, head], dsolved)
        yield
        dcoupling = -mm_nt(dtargets, solved_low)
        dkey_target = dtargets[:, :key_dim]
        dvalue_target = dtargets[:, key_dim:]

        yield
        pair = dcoupling * key_key
        dfade = beta * pair + dscores * scores
        dpair = (jnp.where(strict, dcoupling * (beta * fading), 0.0)).astype(BF)
        dquery_key = (dscores * fading).astype(BF)
        dquery = dquery_fade * grown + mm(dquery_key, key_low)
        fade_rows = jnp.sum(dkey_fade * key_fade, axis=-1, keepdims=True)
        grown_key = grown * keys
        target_rows = jnp.sum(dkey_target * grown_key, axis=-1, keepdims=True)
        dkeys = (
            dkey_fade * rest
            + dkey_target * (beta * grown)
            + mm(dpair, key_low)
            + mm_tn(dpair, key_low)
            + mm_tn(dquery_key, query_low)
        )
        yield
        dvalues = dvalue_target * beta
        dbeta = (
            jnp.sum(pair, axis=-1, keepdims=True)
            + target_rows
            + jnp.sum(dvalue_target * values, axis=-1, keepdims=True)
        )
        row_part = (
            jnp.sum(dfade, axis=-1, keepdims=True)
            + beta * target_rows
            + jnp.sum(dquery_fade * query, axis=-1, keepdims=True) * grown
            - fade_rows
        )
        dlast = dlast + jnp.sum(fade_rows, axis=0, keepdims=True)
        place = lax.broadcasted_iota(jnp.int32, (BLOCK, 1), 0)
        row_part = row_part + jnp.where(place == BLOCK - 1, dlast, 0.0)
        col_row = jnp.sum(dfade, axis=0, keepdims=True)
        results[head] = (row_part, col_row, dbeta)
        yield

        dquery_pre = back_unit(query_pre, query_scale, dquery * factor) * query_slope
        dkey_pre = back_unit(key_pre, key_scale, dkeys) * key_slope
        dext_ref[0:BLOCK, at : at + key_dim] = dquery_pre
        dext_ref[0:BLOCK, at + key_dim : at + 2 * key_dim] = dkey_pre
        dext_ref[0:BLOCK, at + 2 * key_dim : at + head_width] = dvalues * value_slope

    running = [head_work(head) for head in range(heads)]
    while running:
        running = [work for work in running if next(work, 0) is None]

    col_rows = [results[head][1] for head in range(heads)]
    col_part = jnp.concatenate(
        col_rows + [jnp.zeros((HALF - heads, BLOCK), F32)], axis=0
    ).T
    total_grad = -col_part
    small_grad = jnp.zeros((BLOCK, HALF), F32)
    for head in range(heads):
        total_grad = total_grad + jnp.where(lane == head, results[head][0], 0.0)
        small_grad = small_grad + jnp.where(lane == heads + head, results[head][2], 0.0)
    row, col = iota2(BLOCK, BLOCK)
    upper = jnp.where(row <= col, 1.0, 0.0).astype(F32)
    ddecay = mm_exact(upper, total_grad)
    dalpha = ddecay * (-rate_ref[...]) * jax.nn.sigmoid(shifted)
    dsmall_ref[0:1, :] += jnp.sum(ddecay * decays, axis=0, keepdims=True)
    dsmall_ref[1:2, :] += jnp.sum(dalpha, axis=0, keepdims=True)
    draw_ref[:, heads * full_width :] = (
        jnp.where(lane < heads, dalpha, small_grad * betas * (1.0 - betas))
    ).astype(BF)

    width = HALF
    for start in range(0, conv_width, width):
        span = slice(start, start + width)
        grad = dext_ref[0:BLOCK, span]
        acc = taps_ref[3:4, span] * grad
        for tap in range(3):
            acc = acc + taps_ref[tap : tap + 1, span] * dext_ref[pl.ds(3 - tap, BLOCK), span]
        out_at = (start // head_width) * full_width + start % head_width
        draw_ref[:, out_at : out_at + width] = acc.astype(BF)
        for tap in range(4):
            dtaps_ref[tap : tap + 1, span] += jnp.sum(
                grad * ext_ref[pl.ds(5 + tap, BLOCK), span], axis=0, keepdims=True
            )


def mixer_backward(place, part_rows, dmix, weights, saved, taps, rate, bias, onorm, heads):
    hidden, raw, mixed, states, inverses, solved, query_eff, keyw = saved
    rows, width = hidden.shape
    value_dim = onorm.shape[1]
    value_all = heads * value_dim
    conv_width = taps.shape[1]
    key_dim = states.shape[2]
    draw_width = conv_width + value_all + HALF
    steps = rows // BLOCK
    last = steps - 1
    whole = lambda shape, at=0: pl.BlockSpec(shape, lambda i, p: (0,) * (len(shape) - 1) + (at,))
    rows_of = lambda columns, at=0: pl.BlockSpec((BLOCK, columns), lambda i, p: (last - i, at))
    each = lambda a, b: pl.BlockSpec((1, heads, a, b), lambda i, p: (last - i, 0, 0, 0))
    shape = jax.ShapeDtypeStruct
    halo = pl.BlockSpec(
        (8, conv_width), lambda i, p: (jnp.maximum((last - i) * (BLOCK // 8) - 1, 0), 0)
    )

    return pl.pallas_call(
        functools.partial(backward_kernel, heads, SEQ // BLOCK),
        grid_spec=pltpu.PrefetchScalarGridSpec(
            num_scalar_prefetch=1,
            grid=(steps,),
            in_specs=[
                whole((part_rows, width)),
                whole((part_rows, width)),
                whole((part_rows, width)),
                whole((part_rows, width)),
                whole((width, value_all), 1),
                rows_of(conv_width + HALF),
                halo,
                rows_of(width),
                whole((width, value_all), 0),
                rows_of(value_all),
                each(key_dim, value_dim),
                each(BLOCK, BLOCK),
                each(BLOCK, key_dim + value_dim),
                each(BLOCK, key_dim),
                each(key_dim, key_dim),
                whole(taps.shape),
                whole(rate.shape),
                whole(bias.shape),
                whole(onorm.shape),
            ],
            out_specs=[
                rows_of(draw_width),
                whole((8, conv_width)),
                whole((8, HALF)),
                whole((1, value_dim)),
            ],
            scratch_shapes=[
                pltpu.VMEM((heads, key_dim, value_dim), F32),
                pltpu.VMEM((BLOCK + 8, conv_width), F32),
                pltpu.VMEM((BLOCK + 8, conv_width), F32),
                pltpu.VMEM((BLOCK, width), BF),
            ],
        ),
        out_shape=[
            shape((rows, draw_width), BF),
            shape((8, conv_width), F32),
            shape((8, HALF), F32),
            shape((1, value_dim), F32),
        ],
        compiler_params=pltpu.CompilerParams(
            dimension_semantics=("arbitrary",), vmem_limit_bytes=48 * 1024 * 1024
        ),
        cost_estimate=pl.CostEstimate(
            flops=rows * 24_000_000, bytes_accessed=rows * 50_000, transcendentals=0
        ),
        name="mixer_backward",
    )(
        place, *dmix, weights, raw, raw, hidden, weights, mixed, states, inverses, solved,
        query_eff, keyw, taps, rate, bias, onorm,
    )


def dot_plain(left_side, right_side):
    return jnp.dot(left_side, right_side, preferred_element_type=F32)


def dot_right_t(left_side, right_side):
    return lax.dot_general(
        left_side, right_side, (((1,), (1,)), ((), ())), preferred_element_type=F32
    )


def dot_left_t(left_side, right_side):
    return lax.dot_general(
        left_side, right_side, (((0,), (0,)), ((), ())), preferred_element_type=F32
    )


def hop(value, axis, flip):
    count = lax.axis_size(axis)
    return lax.ppermute(value, axis, [(i, i ^ flip) for i in range(count)])


def swap(value, flip):
    return hop(value, "tensor", flip)


def gather_blocks(block):
    far = swap(block, 2)
    near = swap(block, 1)
    return [block, near, far, swap(far, 1)]


def far_sum(parts):
    return (parts[2].astype(F32) + swap(parts[3].astype(BF), 1).astype(F32)).astype(BF)


def scatter_sum(parts):
    far = swap(far_sum(parts), 2).astype(F32)
    near = parts[0].astype(F32) + swap(parts[1].astype(BF), 1).astype(F32)
    return near + far


def by_permutes():
    return lax.axis_size("dp") in (2, 4, 8)


def gather_lines(piece):
    if not by_permutes():
        return [lax.all_gather(piece, "dp", axis=0, tiled=True)]
    return [piece] + [hop(piece, "dp", flip) for flip in range(2, lax.axis_size("dp"), 2)]


def gather_pairs(lines):
    if not by_permutes():
        return lines
    pieces = []
    for line in lines:
        pieces += [line, hop(line, "dp", 1)]
    return pieces


def sum_dp(value):
    return lax.psum_scatter(value, "dp", scatter_dimension=0, tiled=True).astype(F32)


def sum_small(value, axis):
    count = lax.axis_size(axis)
    if count not in (2, 4, 8):
        return lax.psum(value, axis)
    flip = 1
    while flip < count:
        value = value + hop(value, axis, flip)
        flip = 2 * flip
    return value


def pad_columns(value, width):
    return jnp.pad(value, ((0, 0), (0, width - value.shape[1])))


def round_up(value, unit):
    return -(-value // unit) * unit


def by_head(heads, *members):
    columns = []
    for head in range(heads):
        for member in members:
            span = member.shape[1] // heads
            columns.append(member[:, head * span : (head + 1) * span])
    return columns


def per_device(
    tokens,
    cotangent,
    norm1_gain,
    norm2_gain,
    query_weight,
    key_weight,
    value_weight,
    outgate_weight,
    alpha_weight,
    beta_weight,
    conv_query,
    conv_key,
    conv_value,
    decay_log,
    decay_bias,
    onorm_gain,
    output_weight,
    gate_weight,
    up_weight,
    down_weight,
):
    me = lax.axis_index("tensor")
    tensor_count = lax.axis_size("tensor")
    place = me[None].astype(jnp.int32)
    place_dp = lax.axis_index("dp")[None].astype(jnp.int32)
    part_rows = cotangent.shape[0]
    width = tokens.shape[1]
    heads = alpha_weight.shape[1]
    units = gate_weight.shape[1]
    padded = round_up(units, 256)
    key_dim = query_weight.shape[1] // heads
    value_dim = onorm_gain.shape[0]
    value_all = heads * value_dim
    head_width = 2 * key_dim + value_dim

    small = pad_columns(jnp.concatenate([alpha_weight, beta_weight], axis=1), HALF)
    lines = gather_lines(
        jnp.concatenate(
            by_head(heads, query_weight, key_weight, value_weight) + [small], axis=1
        )
    )
    pieces = gather_pairs(lines)
    if len(pieces) == 1:
        place_dp = jnp.zeros_like(place_dp)
    pieces, cot_local, gate_out_local, ffn_local = lax.optimization_barrier(
        (
            pieces,
            cotangent,
            jnp.concatenate([outgate_weight, output_weight.T], axis=1),
            jnp.concatenate(
                [
                    pad_columns(gate_weight, padded),
                    pad_columns(up_weight, padded),
                    pad_columns(down_weight.T, padded),
                ],
                axis=1,
            ),
        )
    )
    w_gate_out = lax.all_gather(gate_out_local, "dp", axis=0, tiled=True)
    w_ffn = lax.all_gather(ffn_local, "dp", axis=0, tiled=True)
    w_pair = w_ffn[:, : 2 * padded]
    w_down_t = w_ffn[:, 2 * padded :]
    cot_blocks = gather_blocks(cot_local)

    taps = jnp.concatenate(by_head(heads, conv_query, conv_key, conv_value), axis=1)
    rate = pad_columns(jnp.exp(decay_log)[None], HALF)
    bias = pad_columns(decay_bias[None], HALF)
    onorm = onorm_gain[None]
    w_first, hidden_one, raw, mixed, *saved = mixer_forward(
        tokens, norm1_gain[None], pieces, place_dp, taps, rate, bias, heads, value_dim
    )
    hidden_one, mixed, cot_far = lax.optimization_barrier((hidden_one, mixed, cot_blocks[2]))
    cot_blocks[2] = cot_far
    normed_blocks, mixer_parts = [None] * 4, [None] * 4
    for first in (3, 1):
        found = gated_out(place, first, part_rows, hidden_one, mixed, w_gate_out, onorm, heads)
        normed_blocks[first], normed_blocks[first - 1] = found[0], found[1]
        mixer_parts[first], mixer_parts[first - 1] = found[2], found[3]
    w_gates = w_gate_out[:, :value_all]
    columns = []
    for head in range(heads):
        columns.append(w_first[:, head * head_width : (head + 1) * head_width])
        columns.append(w_gates[:, head * value_dim : (head + 1) * value_dim])
    columns.append(w_first[:, heads * head_width :])
    w_all = jnp.concatenate(columns, axis=1)

    def block_of(value, flip):
        return lax.dynamic_slice_in_dim(value, (me ^ flip) * part_rows, part_rows, 0)

    mixer_rows = scatter_sum(mixer_parts)
    inputs = block_of(tokens, 0).astype(F32)
    middle = inputs + mixer_rows
    inverse_two = lax.rsqrt(jnp.mean(middle * middle, axis=-1, keepdims=True) + EPS_NORM)
    unit_two = middle * inverse_two
    hidden_blocks = gather_blocks((unit_two * norm2_gain).astype(BF))

    def feed_forward(first, second):
        hidden = jnp.concatenate([hidden_blocks[first], hidden_blocks[second]], axis=0)
        cot = jnp.concatenate([cot_blocks[first], cot_blocks[second]], axis=0)
        pair = dot_plain(hidden, w_pair)
        gate, upward = pair[:, :padded], pair[:, padded:]
        sig = jax.nn.sigmoid(gate)
        silu = gate * sig
        active = (silu * upward).astype(BF)
        active_grad = dot_plain(cot, w_down_t)
        pair_grad = jnp.concatenate(
            [
                (active_grad * upward * (sig * (1.0 + gate * (1.0 - sig)))).astype(BF),
                (active_grad * silu).astype(BF),
            ],
            axis=1,
        )
        hidden_part = dot_right_t(pair_grad, w_pair).astype(BF)
        return hidden, cot, active, pair_grad, hidden_part

    near = feed_forward(1, 0)
    far = feed_forward(3, 2)
    hidden_two_grad = scatter_sum(
        [near[4][part_rows:], near[4][:part_rows], far[4][part_rows:], far[4][:part_rows]]
    )
    gain_two_part = jnp.sum(hidden_two_grad * unit_two, axis=0)
    gained_two = hidden_two_grad * norm2_gain
    middle_grad = (
        cotangent.astype(F32)
        + inverse_two * gained_two
        - unit_two * inverse_two * inverse_two * jnp.mean(middle * gained_two, axis=-1, keepdims=True)
    )
    ffn_grad = jnp.concatenate(
        [
            (dot_left_t(near[0], near[3]) + dot_left_t(far[0], far[3])).astype(BF),
            (dot_left_t(near[1], near[2]) + dot_left_t(far[1], far[2])).astype(BF),
        ],
        axis=1,
    )
    ffn_total = sum_dp(ffn_grad)
    middle_rows, ffn_grad = lax.optimization_barrier((middle_grad.astype(BF), ffn_grad))
    middle_blocks = gather_blocks(middle_rows)
    near_branch = dot_right_t(near[2], w_down_t).astype(BF)
    far_branch = dot_right_t(far[2], w_down_t).astype(BF)
    branch_near = near_branch[part_rows:].astype(F32) + swap(near_branch[:part_rows], 1).astype(F32)
    branch_far = far_sum([None, None, far_branch[part_rows:], far_branch[:part_rows]])
    middle_blocks, branch_near, branch_far, w_all = lax.optimization_barrier(
        (middle_blocks, branch_near, branch_far, w_all)
    )
    block_output = (middle + branch_near + swap(branch_far, 2).astype(F32)).astype(BF)

    draw, dtaps, dsmall, donorm = mixer_backward(
        place,
        part_rows,
        middle_blocks,
        w_gate_out,
        (hidden_one, raw, mixed) + tuple(saved),
        taps,
        rate,
        bias,
        onorm,
        heads,
    )
    output_grad = sum(dot_left_t(block, rows) for block, rows in zip(middle_blocks, normed_blocks))
    weight_grad = dot_left_t(hidden_one, draw)
    gain_one_part = jnp.sum(weight_grad * w_all.astype(F32), axis=1) / norm1_gain
    weight_grad = jnp.concatenate([weight_grad.astype(BF), output_grad.astype(BF)], axis=1)
    weight_grad, draw = lax.optimization_barrier((weight_grad, draw))
    mixer_total = sum_dp(weight_grad)

    def hidden_part(value, flip):
        return dot_right_t(block_of(value, flip), w_all)

    far_low = far_sum([None, None, hidden_part(draw, 2), hidden_part(draw, 3)])
    far_low, draw, gain_one_part = lax.optimization_barrier((far_low, draw, gain_one_part))
    hidden_one_grad = (
        swap(far_low, 2).astype(F32)
        + hidden_part(draw, 0)
        + swap(hidden_part(draw, 1).astype(BF), 1).astype(F32)
    )
    full_width = head_width + value_dim
    output_total = mixer_total[:, draw.shape[1] :]
    smalls = mixer_total[:, heads * full_width : draw.shape[1]]
    totals = [
        mixer_total[:, head * full_width : (head + 1) * full_width] for head in range(heads)
    ]

    inverse_one = lax.rsqrt(jnp.mean(inputs * inputs, axis=-1, keepdims=True) + EPS_NORM)
    unit_one = inputs * inverse_one
    gained = hidden_one_grad * norm1_gain
    tokens_grad = (
        middle_grad
        + inverse_one * gained
        - unit_one * inverse_one * inverse_one * jnp.mean(inputs * gained, axis=-1, keepdims=True)
    )

    tap_count = taps.shape[0]
    shared = sum_small(
        jnp.stack(
            [gain_one_part, gain_two_part, jnp.pad(donorm[0], (0, width - value_dim))]
        ),
        "tensor",
    )
    tap_sums = dtaps[:tap_count]
    table_width = max(tap_sums.shape[1], width)
    table = sum_small(
        jnp.concatenate(
            [
                pad_columns(tap_sums, table_width),
                pad_columns(shared, table_width),
                pad_columns(dsmall[:2], table_width),
            ],
            axis=0,
        ),
        "dp",
    )
    shared = table[tap_count : tap_count + 3]
    own_total = table[tap_count + 3 :]
    gain_share = width // tensor_count
    onorm_share = value_dim // tensor_count

    def collect(values, start, span):
        return jnp.concatenate([value[:, start : start + span] for value in values], axis=1)

    table_heads = [
        table[:tap_count, head * head_width : (head + 1) * head_width] for head in range(heads)
    ]
    return (
        block_output,
        tokens_grad,
        lax.dynamic_slice_in_dim(shared[0], me * gain_share, gain_share, 0),
        lax.dynamic_slice_in_dim(shared[1], me * gain_share, gain_share, 0),
        collect(totals, 0, key_dim),
        collect(totals, key_dim, key_dim),
        collect(totals, 2 * key_dim, value_dim),
        collect(totals, head_width, value_dim),
        smalls[:, :heads],
        smalls[:, heads : 2 * heads],
        collect(table_heads, 0, key_dim),
        collect(table_heads, key_dim, key_dim),
        collect(table_heads, 2 * key_dim, value_dim),
        own_total[0, :heads],
        own_total[1, :heads],
        lax.dynamic_slice_in_dim(shared[2], me * onorm_share, onorm_share, 0),
        output_total.T,
        ffn_total[:, :units],
        ffn_total[:, padded : padded + units],
        ffn_total[:, 2 * padded : 2 * padded + units].T,
    )


def solution(mesh):
    return jax.shard_map(
        per_device,
        mesh=mesh,
        in_specs=(
            P("dp", None),
            P(("dp", "tensor"), None),
            P(),
            P(),
            P("dp", "tensor"),
            P("dp", "tensor"),
            P("dp", "tensor"),
            P("dp", "tensor"),
            P("dp", "tensor"),
            P("dp", "tensor"),
            P(None, "tensor"),
            P(None, "tensor"),
            P(None, "tensor"),
            P("tensor"),
            P("tensor"),
            P(),
            P("tensor", "dp"),
            P("dp", "tensor"),
            P("dp", "tensor"),
            P("tensor", "dp"),
        ),
        out_specs=(
            P(("dp", "tensor"), None),
            P(("dp", "tensor"), None),
            P("tensor"),
            P("tensor"),
            P("dp", "tensor"),
            P("dp", "tensor"),
            P("dp", "tensor"),
            P("dp", "tensor"),
            P("dp", "tensor"),
            P("dp", "tensor"),
            P(None, "tensor"),
            P(None, "tensor"),
            P(None, "tensor"),
            P("tensor"),
            P("tensor"),
            P("tensor"),
            P("tensor", "dp"),
            P("dp", "tensor"),
            P("dp", "tensor"),
            P("tensor", "dp"),
        ),
        check_vma=False,
    )
```

```python
import functools
import jax
import jax.numpy as jnp
from jax import lax
from jax.sharding import PartitionSpec as P
from jax.experimental import pallas as pl
from jax.experimental.pallas import tpu as pltpu

SEQ = 2048
BLOCK = 256
HALF = 128
EPS_NORM = 1e-05
EPS_UNIT = 1e-06
BF = jnp.bfloat16
F32 = jnp.float32


def mm(left, right):
    return lax.dot_general(
        left.astype(BF), right.astype(BF), (((1,), (0,)), ((), ())), preferred_element_type=F32
    )


def mm_nt(left, right):
    return lax.dot_general(
        left.astype(BF), right.astype(BF), (((1,), (1,)), ((), ())), preferred_element_type=F32
    )


def mm_tn(left, right):
    return lax.dot_general(
        left.astype(BF), right.astype(BF), (((0,), (0,)), ((), ())), preferred_element_type=F32
    )


def mm_exact(ones, right):
    first = right.astype(BF)
    rest = right - first.astype(F32)
    second = rest.astype(BF)
    third = (rest - second.astype(F32)).astype(BF)
    return mm(ones, first) + (mm(ones, second) + mm(ones, third))


def iota2(rows, columns):
    return (
        lax.broadcasted_iota(jnp.int32, (rows, columns), 0),
        lax.broadcasted_iota(jnp.int32, (rows, columns), 1),
    )


def unit_lower_inverse(blocks):
    size = blocks[0].shape[0]
    row, col = iota2(size, size)
    eye = jnp.where(row == col, 1.0, 0.0).astype(F32)
    first = jnp.where((row ^ col) == 1, 1.0, 0.0).astype(F32)
    results = [eye - block * first for block in blocks]
    lows = [block.astype(BF) for block in blocks]
    shift = 1
    while (1 << shift) < size:
        mask = jnp.where(((row >> shift) ^ (col >> shift)) == 1, 1.0, 0.0).astype(BF)
        halves = [result.astype(BF) for result in results]
        inner = [mm(low * mask, half).astype(BF) for low, half in zip(lows, halves)]
        results = [
            result - mm(half, part) for result, half, part in zip(results, halves, inner)
        ]
        shift += 1
    return results


def softplus(value):
    return jnp.maximum(value, 0.0) + jnp.log1p(jnp.exp(-jnp.abs(value)))


def lower_ones(size):
    row, col = iota2(size, size)
    return jnp.where(row >= col, 1.0, 0.0).astype(F32)


def fades(total, total_t, index):
    row, col = iota2(BLOCK, BLOCK)
    gaps = total[:, index : index + 1] - total_t[index : index + 1, :]
    fading = jnp.exp(jnp.where(row >= col, gaps, -1e30))
    return fading, row > col


def forward_kernel(
    heads,
    per_seq,
    pieces,
    place_ref,
    x_ref,
    gain_ref,
    taps_ref,
    rate_ref,
    bias_ref,
    *refs,
):
    (
        w_ref,
        hidden_ref,
        raw_ref,
        conv_ref,
        total_ref,
        mixed_ref,
        state_ref,
        inv_ref,
        solved_ref,
        query_eff_ref,
        keyw_ref,
        carry_ref,
        ext_ref,
    ) = refs[pieces:]
    key_dim = state_ref.shape[2]
    value_dim = state_ref.shape[3]
    conv_width = taps_ref.shape[1]
    head_width = conv_width // heads
    step = pl.program_id(0)

    @pl.when(step == 0)
    def _():
        rows = w_ref.shape[0] // pieces
        for index in range(pieces):
            start = pl.multiple_of((place_ref[0] ^ index) * rows, rows)
            w_ref[pl.ds(start, rows), :] = refs[index][...]

    @pl.when(step % per_seq == 0)
    def _():
        carry_ref[...] = jnp.zeros_like(carry_ref)
        ext_ref[0:8, :] = jnp.zeros((8, conv_width), F32)

    @pl.when(step % per_seq != 0)
    def _():
        ext_ref[0:8, :] = ext_ref[BLOCK : BLOCK + 8, :]

    inputs = x_ref[...].astype(F32)
    inverse = lax.rsqrt(jnp.mean(inputs * inputs, axis=-1, keepdims=True) + EPS_NORM)
    hidden = (inputs * inverse * gain_ref[...]).astype(BF)
    hidden_ref[...] = hidden
    ext_ref[8:, :] = mm(hidden, w_ref[:, :conv_width])
    raw_ref[:, :conv_width] = ext_ref[8:, :]
    raw_ref[:, conv_width:] = mm(hidden, w_ref[:, conv_width:])

    small = raw_ref[:, conv_width:]
    betas = jax.nn.sigmoid(small)
    decays = -rate_ref[...] * softplus(small + bias_ref[...])
    total = mm_exact(lower_ones(BLOCK), decays)
    total_ref[...] = total
    total_t = total.T

    def conv(start, width):
        acc = taps_ref[0:1, start : start + width] * ext_ref[pl.ds(5, BLOCK), start : start + width]
        for tap in range(1, 4):
            acc = acc + (
                taps_ref[tap : tap + 1, start : start + width]
                * ext_ref[pl.ds(5 + tap, BLOCK), start : start + width]
            )
        conv_ref[:, start : start + width] = acc
        return acc * jax.nn.sigmoid(acc)

    def unit(value):
        return value * lax.rsqrt(jnp.sum(value * value, axis=-1, keepdims=True) + EPS_UNIT)

    parts = []
    for head in range(heads):
        start = head * head_width
        query = unit(conv(start, key_dim)) * key_dim ** (-0.5)
        keys = unit(conv(start + key_dim, key_dim))
        values = conv(start + 2 * key_dim, value_dim)
        beta = betas[:, heads + head : heads + head + 1]
        fading, strict = fades(total, total_t, head)
        key_low = keys.astype(BF)
        coupling = jnp.where(strict, beta * fading * mm_nt(key_low, key_low), 0.0)
        scores = (mm_nt(query, key_low) * fading).astype(BF)
        parts.append((query, keys, values, beta, coupling, scores))
    blocks = []
    for part in parts:
        coupling = part[4]
        blocks += [coupling[:HALF, :HALF], coupling[HALF:, HALF:]]
    inverses = unit_lower_inverse(blocks)
    for head in range(heads):
        query, keys, values, beta, coupling, scores = parts[head]
        top, bottom = inverses[2 * head], inverses[2 * head + 1]
        cross = -mm(bottom, mm(coupling[HALF:, :HALF], top))
        inverse_low = jnp.concatenate(
            [
                jnp.concatenate([top.astype(BF), jnp.zeros((HALF, HALF), BF)], axis=1),
                jnp.concatenate([cross.astype(BF), bottom.astype(BF)], axis=1),
            ],
            axis=0,
        )
        inv_ref[0, head] = inverse_low
        column = total[:, head : head + 1]
        last = total[BLOCK - 1 :, head : head + 1]
        grown = jnp.exp(column)
        targets = jnp.concatenate(
            [(((beta * grown) * keys)).astype(BF), (beta * values).astype(BF)], axis=1
        )
        solved = mm(inverse_low, targets)
        solved_low = solved.astype(BF)
        solved_ref[0, head] = solved_low
        spread = mm(scores, solved_low)
        query_eff = (query * grown - spread[:, :key_dim]).astype(BF)
        query_eff_ref[0, head] = query_eff
        key_fade = keys * jnp.exp(last - column)
        gathered = mm_tn(key_fade, solved_low)
        keyw = gathered[:, :key_dim].astype(BF)
        keyw_ref[0, head] = keyw
        state = carry_ref[head]
        state_ref[0, head] = state
        state_low = state.astype(BF)
        mixed = mm(query_eff, state_low) + spread[:, key_dim:]
        carry_ref[head] = jnp.exp(last) * state - mm(keyw, state_low) + gathered[:, key_dim:]
        mixed_ref[:, head * value_dim : (head + 1) * value_dim] = mixed


def mixer_forward(tokens, gain, pieces, place, taps, rate, bias, heads, value_dim):
    rows, width = tokens.shape
    total_width = pieces[0].shape[1]
    conv_width = taps.shape[1]
    value_all = heads * value_dim
    key_dim = (conv_width - value_all) // (2 * heads)
    steps = rows // BLOCK
    whole = lambda shape: pl.BlockSpec(shape, lambda i, p: (0,) * len(shape))
    rows_of = lambda columns: pl.BlockSpec((BLOCK, columns), lambda i, p: (i, 0))
    each = lambda a, b: pl.BlockSpec((1, heads, a, b), lambda i, p: (i, 0, 0, 0))
    shape = jax.ShapeDtypeStruct
    return pl.pallas_call(
        functools.partial(forward_kernel, heads, SEQ // BLOCK, len(pieces)),
        grid_spec=pltpu.PrefetchScalarGridSpec(
            num_scalar_prefetch=1,
            grid=(steps,),
            in_specs=[
                rows_of(width),
                whole((1, width)),
                whole(taps.shape),
                whole(rate.shape),
                whole(bias.shape),
            ]
            + [whole(piece.shape) for piece in pieces],
            out_specs=[
                whole((width, total_width)),
                rows_of(width),
                rows_of(total_width),
                rows_of(conv_width),
                rows_of(HALF),
                rows_of(value_all),
                each(key_dim, value_dim),
                each(BLOCK, BLOCK),
                each(BLOCK, key_dim + value_dim),
                each(BLOCK, key_dim),
                each(key_dim, key_dim),
            ],
            scratch_shapes=[
                pltpu.VMEM((heads, key_dim, value_dim), F32),
                pltpu.VMEM((BLOCK + 8, conv_width), F32),
            ],
        ),
        out_shape=[
            shape((width, total_width), BF),
            shape((rows, width), BF),
            shape((rows, total_width), F32),
            shape((rows, conv_width), F32),
            shape((rows, HALF), F32),
            shape((rows, value_all), F32),
            shape((steps, heads, key_dim, value_dim), F32),
            shape((steps, heads, BLOCK, BLOCK), BF),
            shape((steps, heads, BLOCK, key_dim + value_dim), BF),
            shape((steps, heads, BLOCK, key_dim), BF),
            shape((steps, heads, key_dim, key_dim), BF),
        ],
        compiler_params=pltpu.CompilerParams(
            dimension_semantics=("arbitrary",), vmem_limit_bytes=48 * 1024 * 1024
        ),
        cost_estimate=pl.CostEstimate(
            flops=rows * 20_000_000, bytes_accessed=rows * 60_000, transcendentals=0
        ),
        name="mixer_forward",
    )(place, tokens, gain, taps, rate, bias, *pieces)


def gated_kernel(
    heads,
    place_ref,
    hidden_ref,
    mixed_ref,
    wgate_ref,
    wout_ref,
    onorm_ref,
    *out_refs,
):
    value_dim = onorm_ref.shape[1]
    gates = mm(hidden_ref[...], wgate_ref[...])
    columns = []
    for head in range(heads):
        span = slice(head * value_dim, (head + 1) * value_dim)
        mixed = mixed_ref[:, span]
        gate = gates[:, span]
        scale = lax.rsqrt(jnp.mean(mixed * mixed, axis=-1, keepdims=True) + EPS_NORM)
        columns.append(
            (mixed * scale * onorm_ref[...] * (gate * jax.nn.sigmoid(gate))).astype(BF)
        )
    normed = jnp.concatenate(columns, axis=1)
    part = mm_nt(normed, wout_ref[...]).astype(BF)
    for index in range(2):

        @pl.when(pl.program_id(0) == index)
        def _():
            out_refs[index][...] = normed
            out_refs[2 + index][...] = part


def gated_out(place, first, part_rows, hidden, mixed, weights, onorm, heads):
    width = hidden.shape[1]
    value_all = mixed.shape[1]
    whole = lambda block, at: pl.BlockSpec(block, lambda i, p: (0, at))
    theirs = lambda columns: pl.BlockSpec(
        (part_rows, columns), lambda i, p: ((first - i) ^ p[0], 0)
    )
    shape = jax.ShapeDtypeStruct
    return pl.pallas_call(
        functools.partial(gated_kernel, heads),
        grid_spec=pltpu.PrefetchScalarGridSpec(
            num_scalar_prefetch=1,
            grid=(2,),
            in_specs=[
                theirs(width),
                theirs(value_all),
                whole((width, value_all), 0),
                whole((width, value_all), 1),
                whole(onorm.shape, 0),
            ],
            out_specs=[whole((part_rows, value_all), 0)] * 2 + [whole((part_rows, width), 0)] * 2,
        ),
        out_shape=[shape((part_rows, value_all), BF)] * 2 + [shape((part_rows, width), BF)] * 2,
        compiler_params=pltpu.CompilerParams(
            dimension_semantics=("arbitrary",), vmem_limit_bytes=48 * 1024 * 1024
        ),
        cost_estimate=pl.CostEstimate(
            flops=part_rows * 8_000_000, bytes_accessed=part_rows * 24_000, transcendentals=0
        ),
        name="gated_out",
    )(place, hidden, mixed, weights, weights, onorm)


def backward_kernel(
    heads,
    per_seq,
    place_ref,
    *all_refs,
):
    dmix_refs = all_refs[:4]
    (
    wout_ref,
    raw_ref,
    conv_ref,
    total_ref,
    hidden_ref,
    wgate_ref,
    mixed_ref,
    state_ref,
    inv_ref,
    solved_ref,
    query_eff_ref,
    keyw_ref,
    taps_ref,
    rate_ref,
    bias_ref,
    onorm_ref,
    draw_ref,
    dtaps_ref,
    dsmall_ref,
    donorm_ref,
    carry_ref,
    dext_ref,
    dmix_ref,
    ) = all_refs[4:]
    key_dim = state_ref.shape[2]
    value_dim = state_ref.shape[3]
    conv_width = taps_ref.shape[1]
    head_width = conv_width // heads
    gate_at = conv_width + HALF
    step = pl.program_id(0)
    block = pl.num_programs(0) - 1 - step

    per = dmix_refs[0].shape[0] // BLOCK
    source = (block // per) ^ place_ref[0]
    start = pl.multiple_of((block % per) * BLOCK, BLOCK)
    for index in range(4):

        @pl.when(source == index)
        def _():
            dmix_ref[...] = dmix_refs[index][pl.ds(start, BLOCK), :]

    @pl.when(step == 0)
    def _():
        dtaps_ref[...] = jnp.zeros_like(dtaps_ref)
        dsmall_ref[...] = jnp.zeros_like(dsmall_ref)
        donorm_ref[...] = jnp.zeros_like(donorm_ref)

    @pl.when(step % per_seq == 0)
    def _():
        carry_ref[...] = jnp.zeros_like(carry_ref)
        dext_ref[BLOCK:, :] = jnp.zeros((8, conv_width), F32)

    @pl.when(step % per_seq != 0)
    def _():
        dext_ref[BLOCK:, :] = dext_ref[0:8, :]

    small = raw_ref[:, conv_width:]
    betas = jax.nn.sigmoid(small)
    shifted = small + bias_ref[...]
    decays = -rate_ref[...] * softplus(shifted)
    total = total_ref[...]
    total_t = total.T
    lane = lax.broadcasted_iota(jnp.int32, (1, HALF), 1)

    def conv(start, width):
        acc = conv_ref[:, start : start + width]
        sig = jax.nn.sigmoid(acc)
        return acc * sig, sig * (1.0 + acc * (1.0 - sig))

    def back_unit(value, scale, grad):
        along = jnp.sum(value * grad, axis=-1, keepdims=True)
        return scale * grad - value * (scale * scale * scale * along)

    def inv_norm(value):
        return lax.rsqrt(jnp.sum(value * value, axis=-1, keepdims=True) + EPS_UNIT)

    results = {}

    def head_work(head):
        span = slice(head * value_dim, (head + 1) * value_dim)
        at = head * head_width
        grad = mm(dmix_ref[...], wout_ref[:, span])
        gate = mm(hidden_ref[...], wgate_ref[:, span])
        yield
        sig = jax.nn.sigmoid(gate)
        silu = gate * sig
        mixed = mixed_ref[:, span]
        scale = lax.rsqrt(jnp.mean(mixed * mixed, axis=-1, keepdims=True) + EPS_NORM)
        unit_mixed = mixed * scale
        onorm = onorm_ref[...]
        grad_unit = grad * unit_mixed
        donorm_ref[...] += jnp.sum(grad_unit * silu, axis=0, keepdims=True)
        draw_ref[:, gate_at + head * value_dim : gate_at + (head + 1) * value_dim] = (
            grad_unit * onorm * (sig * (1.0 + gate * (1.0 - sig)))
        ).astype(BF)
        grad_on = grad * onorm * silu
        along = jnp.mean(mixed * grad_on, axis=-1, keepdims=True)
        dmixed = scale * grad_on - mixed * (scale * scale * scale * along)
        dmixed_low = dmixed.astype(BF)
        yield

        query_pre, query_slope = conv(at, key_dim)
        key_pre, key_slope = conv(at + key_dim, key_dim)
        values, value_slope = conv(at + 2 * key_dim, value_dim)
        query_scale = inv_norm(query_pre)
        key_scale = inv_norm(key_pre)
        factor = key_dim ** (-0.5)
        query = query_pre * query_scale * factor
        keys = key_pre * key_scale
        beta = betas[:, heads + head : heads + head + 1]
        fading, strict = fades(total, total_t, head)
        query_low = query.astype(BF)
        key_low = keys.astype(BF)
        key_key = jnp.where(strict, mm_nt(key_low, key_low) * fading, 0.0)
        scores = mm_nt(query_low, key_low) * fading
        scores_low = scores.astype(BF)
        column = total[:, head : head + 1]
        last = total[BLOCK - 1 :, head : head + 1]
        grown = jnp.exp(column)
        rest = jnp.exp(last - column)
        key_fade = keys * rest
        key_fade_low = key_fade.astype(BF)
        yield

        state = state_ref[0, head]
        state_low = state.astype(BF)
        dstate = carry_ref[head]
        dstate_low = dstate.astype(BF)
        solved_low = solved_ref[0, head]
        key_part = solved_low[:, :key_dim]
        fresh = solved_low[:, key_dim:].astype(F32) - mm(key_part, state_low)
        fresh_low = fresh.astype(BF)
        yield
        dfresh = mm_tn(scores_low, dmixed_low) + mm(key_fade_low, dstate_low)
        dfresh_low = dfresh.astype(BF)
        yield
        carry_ref[head] = (
            jnp.exp(last) * dstate
            - mm_tn(keyw_ref[0, head], dstate_low)
            + mm_tn(query_eff_ref[0, head], dmixed_low)
        )
        dlast = jnp.exp(last) * jnp.sum(
            jnp.sum(state * dstate, axis=1, keepdims=True), axis=0, keepdims=True
        )
        yield
        dscores = mm_nt(dmixed_low, fresh_low)
        dquery_fade = mm_nt(dmixed_low, state_low)
        dkey_fade = mm_nt(fresh_low, dstate_low)
        dkey_part = -mm_nt(dfresh_low, state_low)
        yield
        dsolved = jnp.concatenate([dkey_part.astype(BF), dfresh_low], axis=1)
        dtargets = mm_tn(inv_ref[0, head], dsolved)
        yield
        dcoupling = -mm_nt(dtargets, solved_low)
        dkey_target = dtargets[:, :key_dim]
        dvalue_target = dtargets[:, key_dim:]

        yield
        pair = dcoupling * key_key
        dfade = beta * pair + dscores * scores
        dpair = (jnp.where(strict, dcoupling * (beta * fading), 0.0)).astype(BF)
        dquery_key = (dscores * fading).astype(BF)
        dquery = dquery_fade * grown + mm(dquery_key, key_low)
        fade_rows = jnp.sum(dkey_fade * key_fade, axis=-1, keepdims=True)
        grown_key = grown * keys
        target_rows = jnp.sum(dkey_target * grown_key, axis=-1, keepdims=True)
        dkeys = (
            dkey_fade * rest
            + dkey_target * (beta * grown)
            + mm(dpair, key_low)
            + mm_tn(dpair, key_low)
            + mm_tn(dquery_key, query_low)
        )
        yield
        dvalues = dvalue_target * beta
        dbeta = (
            jnp.sum(pair, axis=-1, keepdims=True)
            + target_rows
            + jnp.sum(dvalue_target * values, axis=-1, keepdims=True)
        )
        row_part = (
            jnp.sum(dfade, axis=-1, keepdims=True)
            + beta * target_rows
            + jnp.sum(dquery_fade * query, axis=-1, keepdims=True) * grown
            - fade_rows
        )
        dlast = dlast + jnp.sum(fade_rows, axis=0, keepdims=True)
        place = lax.broadcasted_iota(jnp.int32, (BLOCK, 1), 0)
        row_part = row_part + jnp.where(place == BLOCK - 1, dlast, 0.0)
        col_row = jnp.sum(dfade, axis=0, keepdims=True)
        results[head] = (row_part, col_row, dbeta)
        yield

        dquery_pre = back_unit(query_pre, query_scale, dquery * factor) * query_slope
        dkey_pre = back_unit(key_pre, key_scale, dkeys) * key_slope
        dext_ref[0:BLOCK, at : at + key_dim] = dquery_pre
        dext_ref[0:BLOCK, at + key_dim : at + 2 * key_dim] = dkey_pre
        dext_ref[0:BLOCK, at + 2 * key_dim : at + head_width] = dvalues * value_slope

    running = [head_work(head) for head in range(heads)]
    while running:
        running = [work for work in running if next(work, 0) is None]

    col_rows = [results[head][1] for head in range(heads)]
    col_part = jnp.concatenate(
        col_rows + [jnp.zeros((HALF - heads, BLOCK), F32)], axis=0
    ).T
    total_grad = -col_part
    small_grad = jnp.zeros((BLOCK, HALF), F32)
    for head in range(heads):
        total_grad = total_grad + jnp.where(lane == head, results[head][0], 0.0)
        small_grad = small_grad + jnp.where(lane == heads + head, results[head][2], 0.0)
    row, col = iota2(BLOCK, BLOCK)
    upper = jnp.where(row <= col, 1.0, 0.0).astype(F32)
    ddecay = mm_exact(upper, total_grad)
    dalpha = ddecay * (-rate_ref[...]) * jax.nn.sigmoid(shifted)
    dsmall_ref[0:1, :] += jnp.sum(ddecay * decays, axis=0, keepdims=True)
    dsmall_ref[1:2, :] += jnp.sum(dalpha, axis=0, keepdims=True)
    draw_ref[:, conv_width:gate_at] = (
        jnp.where(lane < heads, dalpha, small_grad * betas * (1.0 - betas))
    ).astype(BF)

    width = HALF
    for start in range(0, conv_width, width):
        span = slice(start, start + width)
        raw = raw_ref[:, span]
        acc = jnp.zeros((BLOCK, width), F32)
        for tap in range(4):
            grad = dext_ref[pl.ds(3 - tap, BLOCK), span]
            acc = acc + taps_ref[tap : tap + 1, span] * grad
            dtaps_ref[tap : tap + 1, span] += jnp.sum(grad * raw, axis=0, keepdims=True)
        draw_ref[:, span] = acc.astype(BF)


def mixer_backward(place, part_rows, dmix, weights, saved, taps, rate, bias, onorm, heads):
    hidden, raw, conv, total, mixed, states, inverses, solved, query_eff, keyw = saved
    rows, width = hidden.shape
    value_dim = onorm.shape[1]
    value_all = heads * value_dim
    conv_width = taps.shape[1]
    key_dim = states.shape[2]
    draw_width = conv_width + value_all + HALF
    steps = rows // BLOCK
    last = steps - 1
    whole = lambda shape, at=0: pl.BlockSpec(shape, lambda i, p: (0,) * (len(shape) - 1) + (at,))
    rows_of = lambda columns, at=0: pl.BlockSpec((BLOCK, columns), lambda i, p: (last - i, at))
    each = lambda a, b: pl.BlockSpec((1, heads, a, b), lambda i, p: (last - i, 0, 0, 0))
    shape = jax.ShapeDtypeStruct
    return pl.pallas_call(
        functools.partial(backward_kernel, heads, SEQ // BLOCK),
        grid_spec=pltpu.PrefetchScalarGridSpec(
            num_scalar_prefetch=1,
            grid=(steps,),
            in_specs=[
                whole((part_rows, width)),
                whole((part_rows, width)),
                whole((part_rows, width)),
                whole((part_rows, width)),
                whole((width, value_all), 1),
                rows_of(conv_width + HALF),
                rows_of(conv_width),
                rows_of(HALF),
                rows_of(width),
                whole((width, value_all), 0),
                rows_of(value_all),
                each(key_dim, value_dim),
                each(BLOCK, BLOCK),
                each(BLOCK, key_dim + value_dim),
                each(BLOCK, key_dim),
                each(key_dim, key_dim),
                whole(taps.shape),
                whole(rate.shape),
                whole(bias.shape),
                whole(onorm.shape),
            ],
            out_specs=[
                rows_of(draw_width),
                whole((8, conv_width)),
                whole((8, HALF)),
                whole((1, value_dim)),
            ],
            scratch_shapes=[
                pltpu.VMEM((heads, key_dim, value_dim), F32),
                pltpu.VMEM((BLOCK + 8, conv_width), F32),
                pltpu.VMEM((BLOCK, width), BF),
            ],
        ),
        out_shape=[
            shape((rows, draw_width), BF),
            shape((8, conv_width), F32),
            shape((8, HALF), F32),
            shape((1, value_dim), F32),
        ],
        compiler_params=pltpu.CompilerParams(
            dimension_semantics=("arbitrary",), vmem_limit_bytes=48 * 1024 * 1024
        ),
        cost_estimate=pl.CostEstimate(
            flops=rows * 2_000_000, bytes_accessed=rows * 5_000, transcendentals=0
        ),
        name="mixer_backward",
    )(
        place, *dmix, weights, raw, conv, total, hidden, weights, mixed, states, inverses, solved,
        query_eff, keyw, taps, rate, bias, onorm,
    )


def dot_plain(left_side, right_side):
    return jnp.dot(left_side, right_side, preferred_element_type=F32)


def dot_right_t(left_side, right_side):
    return lax.dot_general(
        left_side, right_side, (((1,), (1,)), ((), ())), preferred_element_type=F32
    )


def dot_left_t(left_side, right_side):
    return lax.dot_general(
        left_side, right_side, (((0,), (0,)), ((), ())), preferred_element_type=F32
    )


def hop(value, axis, flip):
    count = lax.axis_size(axis)
    return lax.ppermute(value, axis, [(i, i ^ flip) for i in range(count)])


def swap(value, flip):
    return hop(value, "tensor", flip)


def gather_blocks(block):
    far = swap(block, 2)
    near = swap(block, 1)
    return [block, near, far, swap(far, 1)]


def far_sum(parts):
    return (parts[2].astype(F32) + swap(parts[3].astype(BF), 1).astype(F32)).astype(BF)


def scatter_sum(parts):
    far = swap(far_sum(parts), 2).astype(F32)
    near = parts[0].astype(F32) + swap(parts[1].astype(BF), 1).astype(F32)
    return near + far


def by_permutes():
    return lax.axis_size("dp") in (2, 4, 8)


def gather_lines(piece):
    if not by_permutes():
        return [lax.all_gather(piece, "dp", axis=0, tiled=True)]
    return [piece] + [hop(piece, "dp", flip) for flip in range(2, lax.axis_size("dp"), 2)]


def gather_pairs(lines):
    if not by_permutes():
        return lines
    pieces = []
    for line in lines:
        pieces += [line, hop(line, "dp", 1)]
    return pieces


def sum_dp(value):
    return lax.psum_scatter(value, "dp", scatter_dimension=0, tiled=True).astype(F32)


def sum_small(value, axis):
    count = lax.axis_size(axis)
    if count not in (2, 4, 8):
        return lax.psum(value, axis)
    flip = 1
    while flip < count:
        value = value + hop(value, axis, flip)
        flip = 2 * flip
    return value


def pad_columns(value, width):
    return jnp.pad(value, ((0, 0), (0, width - value.shape[1])))


def round_up(value, unit):
    return -(-value // unit) * unit


def by_head(heads, *members):
    columns = []
    for head in range(heads):
        for member in members:
            span = member.shape[1] // heads
            columns.append(member[:, head * span : (head + 1) * span])
    return columns


def per_device(
    tokens,
    cotangent,
    norm1_gain,
    norm2_gain,
    query_weight,
    key_weight,
    value_weight,
    outgate_weight,
    alpha_weight,
    beta_weight,
    conv_query,
    conv_key,
    conv_value,
    decay_log,
    decay_bias,
    onorm_gain,
    output_weight,
    gate_weight,
    up_weight,
    down_weight,
):
    me = lax.axis_index("tensor")
    tensor_count = lax.axis_size("tensor")
    place = me[None].astype(jnp.int32)
    place_dp = lax.axis_index("dp")[None].astype(jnp.int32)
    part_rows = cotangent.shape[0]
    width = tokens.shape[1]
    heads = alpha_weight.shape[1]
    units = gate_weight.shape[1]
    padded = round_up(units, 256)
    key_dim = query_weight.shape[1] // heads
    value_dim = onorm_gain.shape[0]
    value_all = heads * value_dim
    head_width = 2 * key_dim + value_dim

    small = pad_columns(jnp.concatenate([alpha_weight, beta_weight], axis=1), HALF)
    lines = gather_lines(
        jnp.concatenate(
            by_head(heads, query_weight, key_weight, value_weight) + [small], axis=1
        )
    )
    pieces = gather_pairs(lines)
    if len(pieces) == 1:
        place_dp = jnp.zeros_like(place_dp)
    pieces, cot_local, gate_out_local, ffn_local = lax.optimization_barrier(
        (
            pieces,
            cotangent,
            jnp.concatenate([outgate_weight, output_weight.T], axis=1),
            jnp.concatenate(
                [
                    pad_columns(gate_weight, padded),
                    pad_columns(up_weight, padded),
                    pad_columns(down_weight.T, padded),
                ],
                axis=1,
            ),
        )
    )
    w_gate_out = lax.all_gather(gate_out_local, "dp", axis=0, tiled=True)
    w_ffn = lax.all_gather(ffn_local, "dp", axis=0, tiled=True)
    w_pair = w_ffn[:, : 2 * padded]
    w_down_t = w_ffn[:, 2 * padded :]
    cot_blocks = gather_blocks(cot_local)

    taps = jnp.concatenate(by_head(heads, conv_query, conv_key, conv_value), axis=1)
    rate = pad_columns(jnp.exp(decay_log)[None], HALF)
    bias = pad_columns(decay_bias[None], HALF)
    onorm = onorm_gain[None]
    w_first, hidden_one, raw, conv_rows, totals, mixed, *saved = mixer_forward(
        tokens, norm1_gain[None], pieces, place_dp, taps, rate, bias, heads, value_dim
    )
    hidden_one, mixed, cot_far = lax.optimization_barrier((hidden_one, mixed, cot_blocks[2]))
    cot_blocks[2] = cot_far
    normed_blocks, mixer_parts = [None] * 4, [None] * 4
    for first in (3, 1):
        found = gated_out(place, first, part_rows, hidden_one, mixed, w_gate_out, onorm, heads)
        normed_blocks[first], normed_blocks[first - 1] = found[0], found[1]
        mixer_parts[first], mixer_parts[first - 1] = found[2], found[3]
    def block_of(value, flip):
        return lax.dynamic_slice_in_dim(value, (me ^ flip) * part_rows, part_rows, 0)

    mixer_rows = scatter_sum(mixer_parts)
    inputs = block_of(tokens, 0).astype(F32)
    middle = inputs + mixer_rows
    inverse_two = lax.rsqrt(jnp.mean(middle * middle, axis=-1, keepdims=True) + EPS_NORM)
    unit_two = middle * inverse_two
    hidden_blocks = gather_blocks((unit_two * norm2_gain).astype(BF))

    def feed_forward(first, second):
        hidden = jnp.concatenate([hidden_blocks[first], hidden_blocks[second]], axis=0)
        cot = jnp.concatenate([cot_blocks[first], cot_blocks[second]], axis=0)
        pair = dot_plain(hidden, w_pair)
        gate, upward = pair[:, :padded], pair[:, padded:]
        sig = jax.nn.sigmoid(gate)
        silu = gate * sig
        active = (silu * upward).astype(BF)
        active_grad = dot_plain(cot, w_down_t)
        pair_grad = jnp.concatenate(
            [
                (active_grad * upward * (sig * (1.0 + gate * (1.0 - sig)))).astype(BF),
                (active_grad * silu).astype(BF),
            ],
            axis=1,
        )
        hidden_part = dot_right_t(pair_grad, w_pair).astype(BF)
        return hidden, cot, active, pair_grad, hidden_part

    near = feed_forward(1, 0)
    far = feed_forward(3, 2)
    hidden_two_grad = scatter_sum(
        [near[4][part_rows:], near[4][:part_rows], far[4][part_rows:], far[4][:part_rows]]
    )
    gain_two_part = jnp.sum(hidden_two_grad * unit_two, axis=0)
    gained_two = hidden_two_grad * norm2_gain
    middle_grad = (
        cotangent.astype(F32)
        + inverse_two * gained_two
        - unit_two * inverse_two * inverse_two * jnp.mean(middle * gained_two, axis=-1, keepdims=True)
    )
    ffn_grad = jnp.concatenate(
        [
            (dot_left_t(near[0], near[3]) + dot_left_t(far[0], far[3])).astype(BF),
            (dot_left_t(near[1], near[2]) + dot_left_t(far[1], far[2])).astype(BF),
        ],
        axis=1,
    )
    ffn_total = sum_dp(ffn_grad)
    middle_rows, ffn_grad = lax.optimization_barrier((middle_grad.astype(BF), ffn_grad))
    middle_blocks = gather_blocks(middle_rows)
    draw, dtaps, dsmall, donorm = mixer_backward(
        place,
        part_rows,
        middle_blocks,
        w_gate_out,
        (hidden_one, raw, conv_rows, totals, mixed) + tuple(saved),
        taps,
        rate,
        bias,
        onorm,
        heads,
    )
    output_grad = sum(dot_left_t(block, rows) for block, rows in zip(middle_blocks, normed_blocks))
    weight_grad = dot_left_t(hidden_one, draw)
    weight_grad = jnp.concatenate([weight_grad.astype(BF), output_grad.astype(BF)], axis=1)
    weight_grad, draw, near_active, far_active, w_first = lax.optimization_barrier(
        (weight_grad, draw, near[2], far[2], w_first)
    )
    mixer_total = sum_dp(weight_grad)
    w_gates = w_gate_out[:, :value_all]
    gate_at = w_first.shape[1]

    def hidden_part(value, flip):
        rows = block_of(value, flip)
        return dot_right_t(rows[:, :gate_at], w_first) + dot_right_t(rows[:, gate_at:], w_gates)

    far_low = far_sum([None, None, hidden_part(draw, 2), hidden_part(draw, 3)])
    far_low, draw, near_active, far_active, weight_grad = lax.optimization_barrier(
        (far_low, draw, near_active, far_active, weight_grad)
    )
    gain_one_part = (
        jnp.sum(weight_grad[:, :gate_at].astype(F32) * w_first.astype(F32), axis=1)
        + jnp.sum(
            weight_grad[:, gate_at : draw.shape[1]].astype(F32) * w_gates.astype(F32), axis=1
        )
    ) / norm1_gain
    near_branch = dot_right_t(near_active, w_down_t).astype(BF)
    far_branch = dot_right_t(far_active, w_down_t).astype(BF)
    far_term = swap(far_low, 2)
    hidden_one_grad = (
        far_term.astype(F32)
        + hidden_part(draw, 0)
        + swap(hidden_part(draw, 1).astype(BF), 1).astype(F32)
    )
    far_term, near_branch, far_branch = lax.optimization_barrier(
        (far_term, near_branch, far_branch)
    )
    branch_rows = scatter_sum(
        [
            near_branch[part_rows:],
            near_branch[:part_rows],
            far_branch[part_rows:],
            far_branch[:part_rows],
        ]
    )
    block_output = (middle + branch_rows).astype(BF)
    output_total = mixer_total[:, draw.shape[1] :]
    smalls = mixer_total[:, heads * head_width : gate_at]
    head_totals = [
        mixer_total[:, head * head_width : (head + 1) * head_width] for head in range(heads)
    ]

    inverse_one = lax.rsqrt(jnp.mean(inputs * inputs, axis=-1, keepdims=True) + EPS_NORM)
    unit_one = inputs * inverse_one
    gained = hidden_one_grad * norm1_gain
    tokens_grad = (
        middle_grad
        + inverse_one * gained
        - unit_one * inverse_one * inverse_one * jnp.mean(inputs * gained, axis=-1, keepdims=True)
    )

    tap_count = taps.shape[0]
    shared = sum_small(
        jnp.stack(
            [gain_one_part, gain_two_part, jnp.pad(donorm[0], (0, width - value_dim))]
        ),
        "tensor",
    )
    tap_sums = dtaps[:tap_count]
    table_width = max(tap_sums.shape[1], width)
    table = sum_small(
        jnp.concatenate(
            [
                pad_columns(tap_sums, table_width),
                pad_columns(shared, table_width),
                pad_columns(dsmall[:2], table_width),
            ],
            axis=0,
        ),
        "dp",
    )
    shared = table[tap_count : tap_count + 3]
    own_total = table[tap_count + 3 :]
    gain_share = width // tensor_count
    onorm_share = value_dim // tensor_count

    def collect(values, start, span):
        return jnp.concatenate([value[:, start : start + span] for value in values], axis=1)

    table_heads = [
        table[:tap_count, head * head_width : (head + 1) * head_width] for head in range(heads)
    ]
    return (
        block_output,
        tokens_grad,
        lax.dynamic_slice_in_dim(shared[0], me * gain_share, gain_share, 0),
        lax.dynamic_slice_in_dim(shared[1], me * gain_share, gain_share, 0),
        collect(head_totals, 0, key_dim),
        collect(head_totals, key_dim, key_dim),
        collect(head_totals, 2 * key_dim, value_dim),
        mixer_total[:, gate_at : draw.shape[1]],
        smalls[:, :heads],
        smalls[:, heads : 2 * heads],
        collect(table_heads, 0, key_dim),
        collect(table_heads, key_dim, key_dim),
        collect(table_heads, 2 * key_dim, value_dim),
        own_total[0, :heads],
        own_total[1, :heads],
        lax.dynamic_slice_in_dim(shared[2], me * onorm_share, onorm_share, 0),
        output_total.T,
        ffn_total[:, :units],
        ffn_total[:, padded : padded + units],
        ffn_total[:, 2 * padded : 2 * padded + units].T,
    )


def solution(mesh):
    return jax.shard_map(
        per_device,
        mesh=mesh,
        in_specs=(
            P("dp", None),
            P(("dp", "tensor"), None),
            P(),
            P(),
            P("dp", "tensor"),
            P("dp", "tensor"),
            P("dp", "tensor"),
            P("dp", "tensor"),
            P("dp", "tensor"),
            P("dp", "tensor"),
            P(None, "tensor"),
            P(None, "tensor"),
            P(None, "tensor"),
            P("tensor"),
            P("tensor"),
            P(),
            P("tensor", "dp"),
            P("dp", "tensor"),
            P("dp", "tensor"),
            P("tensor", "dp"),
        ),
        out_specs=(
            P(("dp", "tensor"), None),
            P(("dp", "tensor"), None),
            P("tensor"),
            P("tensor"),
            P("dp", "tensor"),
            P("dp", "tensor"),
            P("dp", "tensor"),
            P("dp", "tensor"),
            P("dp", "tensor"),
            P("dp", "tensor"),
            P(None, "tensor"),
            P(None, "tensor"),
            P(None, "tensor"),
            P("tensor"),
            P("tensor"),
            P("tensor"),
            P("tensor", "dp"),
            P("dp", "tensor"),
            P("dp", "tensor"),
            P("tensor", "dp"),
        ),
        check_vma=False,
    )
```
